256 devices in a mesh: gx: 8 (over y, core), gy: 32 (over x, z).
Axes of the slice: x: 4, y: 4, z: 8, core: 2. Of those that a mesh axis runs over, the one named last changes fastest.
Arguments:
- field: bfloat16 [1024, 256, 512], P('gx', 'gy'), may hold values from -6 to 6
- conv_weight: bfloat16 [27, 32, 32], replicated, may hold values from -0.21875 to 0.21875
- conv_bias: float32 [32], replicated, may hold values from -3 to 3
- spectral_weight: bfloat16 [32, 2, 32, 32], replicated, may hold values from -2 to 2
Outputs:
- layer_out: bfloat16 [1024, 256, 512], P('gx', 'gy')
The draws below stay inside these ranges and needn't reach their ends.
All inputs are finite; a program needn't handle non-finite values.
Results may differ from the reference program's by a relative error of at most 0.0049.
Values may be sent and summed in bfloat16 or wider, within the bound.
A program may use at most 128 MiB of HBM per device.

```python
import math
import jax
import jax.numpy as jnp
from jax import lax

C = 32
M = 32
NZ = 16
NX = 1024
NY = 256
ZC = 512


def block_scale(rng, dims, split, low, high):
    def one(dim, parts):
        steps = jax.random.uniform(jax.random.fold_in(jax.random.fold_in(rng, 6), dim), (parts,), jnp.float32, low / len(split), high / len(split))
        return jnp.repeat(jnp.exp(steps), dims[dim] // parts).reshape((-1,) + (1,) * (len(dims) - dim - 1))

    gain = one(*split[0])
    for cut in split[1:]:
        gain = gain * one(*cut)
    return gain


def normal_values(own_key, extent, scale, most, shards=(), kind=jnp.bfloat16):
    factor_of = block_scale(own_key, extent, shards, -0.22, 0.18) if shards else 1.0
    values = jax.random.normal(own_key, extent, jnp.float32) * scale * factor_of
    return jnp.minimum(jnp.maximum(values, -most), most).astype(kind)


def setup_inputs(seed: int = 0) -> dict:
    streams_of = jax.random.split(jax.random.key(seed), 5)
    return {
        "field": normal_values(streams_of[0], (NX, NY, ZC), 1.0, 6.0, ((0, 8), (1, 32))),
        "conv_weight": normal_values(streams_of[1], (27, C, C), (27 * C) ** -0.5, 0.21875),
        "conv_bias": normal_values(streams_of[2], (C,), 0.5, 3.0, (), jnp.float32),
        "spectral_weight": normal_values(streams_of[3], (M, 2, C, C), (C // 4) ** -0.5, 2.0),
    }


def make_tables(length, mode_count, first, count):
    positions = first + jnp.arange(count, dtype=jnp.int32)
    mode_ids = jnp.arange(mode_count, dtype=jnp.int32)
    turns = mode_ids[:, None] * positions[None, :] % length
    angles = turns.astype(jnp.float32) * (2.0 * math.pi / length)
    normalizer = 1.0 / math.sqrt(length)
    pairs = jnp.stack([jnp.cos(angles), -jnp.sin(angles)], axis=1) * normalizer
    doubling = jnp.where(mode_ids == 0, 1.0, 2.0).astype(jnp.float32)
    forward_table = pairs.reshape(2 * mode_count, count).astype(jnp.bfloat16)
    inverse_table = (pairs * doubling[:, None, None]).reshape(2 * mode_count, count).T.astype(jnp.bfloat16)
    return (forward_table, inverse_table)

def mixing_kernel(spectral_weight):
    real_part = spectral_weight[:, 0]
    imag_part = spectral_weight[:, 1]
    upper = jnp.stack([real_part, imag_part], axis=1)
    lower = jnp.stack([-imag_part, real_part], axis=1)
    return jnp.stack([upper, lower], axis=1)

def reference(field, conv_weight, conv_bias, spectral_weight):
    volume = field.astype(jnp.float32).reshape(1, NX, NY, NZ, C)
    kernel = conv_weight.astype(jnp.float32).reshape(3, 3, 3, C, C)
    conv = lax.conv_general_dilated(volume, kernel, (1, 1, 1), 'SAME', dimension_numbers=('NHWDC', 'HWDIO', 'NHWDC'), precision=lax.Precision.HIGHEST)
    conv = conv.reshape(NX, NY, ZC)
    forward_table, inverse_table = make_tables(NX, M, 0, NX)
    columns = field.reshape(NX, NY * ZC)
    coef = jnp.dot(forward_table, columns, preferred_element_type=jnp.float32).astype(jnp.bfloat16)
    coef = coef.reshape(M, 2, NY * NZ, C)
    mixed = jnp.einsum('mrpc,mrqco->mqpo', coef.astype(jnp.float32), mixing_kernel(spectral_weight).astype(jnp.float32), precision=lax.Precision.HIGHEST).astype(jnp.bfloat16)
    mixed = mixed.reshape(2 * M, NY * ZC)
    spectral = jnp.dot(inverse_table, mixed, preferred_element_type=jnp.float32).reshape(NX, NY, ZC)
    total = conv + spectral + jnp.tile(conv_bias, NZ)
    return jax.nn.gelu(total, approximate=False).astype(jnp.bfloat16)
```

```python
import functools
import math

import jax
import jax.numpy as jnp
import numpy as np
from jax import lax
from jax.experimental import pallas as pl
from jax.experimental.pallas import tpu as pltpu
from jax.sharding import PartitionSpec as P

MESH = pl.DeviceIdType.MESH
CHUNKS = 2
F32 = jnp.float32
BF16 = jnp.bfloat16


def dot(a, b):
    return jnp.dot(a, b, preferred_element_type=F32)


def expanded_tables(length, modes, groups, rows_y):
    turns = (np.arange(modes)[:, None] * np.arange(length)[None, :]) % length
    angles = turns.astype(np.float32) * np.float32(2.0 * math.pi / length)
    pairs = np.stack([np.cos(angles), -np.sin(angles)], axis=1) * np.float32(1.0 / math.sqrt(length))
    doubling = np.where(np.arange(modes) == 0, 1.0, 2.0).astype(np.float32)
    forward = pairs.reshape(2 * modes, groups, length // groups).transpose(1, 0, 2)
    inverse = (pairs * doubling[:, None, None]).reshape(2 * modes, groups, length // groups).transpose(1, 2, 0)
    forward = np.repeat(forward, rows_y, axis=2)
    inverse = np.repeat(inverse, rows_y, axis=2)
    return jnp.asarray(forward, BF16), jnp.asarray(inverse, BF16)


def spread(table_ref, out_ref):
    rows, lanes = table_ref.shape

    def body(i, carry):
        part = table_ref[pl.ds(pl.multiple_of(i * 16, 16), 16), :].astype(F32)
        wide = jnp.broadcast_to(part[:, None, :], (16, 8, lanes))
        keep = lax.broadcasted_iota(jnp.int32, (16, 8, lanes), 1) == (
            lax.broadcasted_iota(jnp.int32, (16, 8, lanes), 2) & 7
        )
        out_ref[pl.ds(pl.multiple_of(i * 128, 128), 128), :] = (
            jnp.where(keep, wide, 0.0).reshape(128, lanes).astype(BF16)
        )
        return carry

    lax.fori_loop(0, rows // 16, body, 0)


def layer_kernel(
    field, convw, bias, specw, ftab, itab, out,
    fs, fexp, iexp, cw, sw, bv, amat, gmat, wrep, tmat, cmat, rmat, conv,
    part, cbuf, cland, sbuf, rland, mixed, ybuf, yland, xland, cornl,
    load_sem, bar_send, c_send, c_recv, r_send, r_recv, a_send, a_recv, f_send, f_recv,
    x_send, x_recv, y_send, y_recv, k_send, k_recv,
):
    nch, _, lc = mixed.shape
    tiles = lc // 128
    g = lax.axis_index("gx")
    h = lax.axis_index("gy")
    ng = lax.axis_size("gx")
    nh = lax.axis_size("gy")
    ny = ng // 2
    yc, core = g // 2, g % 2
    q = core * ny + yc
    sib = (2 * yc + (1 - core), h)

    def ychip(j):
        return (2 * lax.rem(yc + j, ny) + core, h)

    left, right = lax.rem(g + ng - 1, ng), lax.rem(g + 1, ng)
    prev, nxt = lax.rem(h + nh - 1, nh), lax.rem(h + 1, nh)
    outer = lax.rem(g + ng + 2 * core - 1, ng)

    def remote(src, dst, s, r, dev):
        return pltpu.make_async_remote_copy(
            src_ref=src, dst_ref=dst, send_sem=s, recv_sem=r, device_id=dev, device_id_type=MESH
        )

    barrier = pltpu.get_barrier_semaphore()
    partners = [sib] + [ychip(j) for j in range(1, ny)] + [(outer, h), (g, prev), (g, nxt)]
    for dev in partners:
        pl.semaphore_signal(barrier, inc=1, device_id=dev, device_id_type=MESH)

    load_f = pltpu.make_async_copy(ftab.at[g], fexp, load_sem.at[0])
    load_x = pltpu.make_async_copy(field, fs.at[1, pl.ds(1, 128)], load_sem.at[1])
    load_i = pltpu.make_async_copy(itab.at[g], iexp, load_sem.at[2])
    load_w = pltpu.make_async_copy(convw, cw, load_sem.at[3])
    load_s = pltpu.make_async_copy(specw.at[pl.ds(4 * q, 4)], sw, load_sem.at[4])
    load_b = pltpu.make_async_copy(bias, bv, load_sem.at[5])
    for load in (load_f, load_x, load_w, load_s, load_i, load_b):
        load.start()

    load_f.wait()
    spread(fexp, amat)
    load_x.wait()
    pl.semaphore_wait(barrier, len(partners))
    x_copies = [
        remote(fs.at[1, pl.ds(127, 2)], xland.at[0], x_send.at[0], x_recv.at[0], (right, h)),
        remote(fs.at[1, pl.ds(1, 2)], xland.at[1], x_send.at[1], x_recv.at[1], (left, h)),
    ]
    for copy in x_copies:
        copy.start()
    c_copies = []
    own_rows = pl.ds(pl.multiple_of(core * 256, 256), 256)
    sib_rows = pl.ds(pl.multiple_of((1 - core) * 256, 256), 256)
    for ch in range(nch):
        cells = fs[1, 1:129, :, ch * lc : (ch + 1) * lc].reshape(1024, lc)
        part[ch] = dot(amat[...], cells)
        cbuf[ch] = part[ch, sib_rows, :].astype(BF16)
        copy = remote(cbuf.at[ch], cland.at[ch], c_send.at[ch], c_recv.at[ch], sib)
        copy.start()
        c_copies.append(copy)

    row = lax.broadcasted_iota(jnp.int32, (64, 256), 0)
    col = lax.broadcasted_iota(jnp.int32, (64, 256), 1)
    pick = jnp.where(col == (row & 31) * 8 + jnp.where(row < 32, 7, 0), 1.0, 0.0).astype(BF16)
    for b in range(4):
        cells = fs[1, 1 + 32 * b : 33 + 32 * b].reshape(256, 512)
        picked = dot(pick, cells).astype(BF16)
        ybuf[0, 32 * b : 32 * b + 32, :] = picked[:32]
        ybuf[1, 32 * b : 32 * b + 32, :] = picked[32:]
    y_copies = [
        remote(ybuf.at[0], yland.at[0], y_send.at[0], y_recv.at[0], (g, nxt)),
        remote(ybuf.at[1], yland.at[1], y_send.at[1], y_recv.at[1], (g, prev)),
    ]
    for copy in y_copies:
        copy.start()

    load_s.wait()
    rep4 = jnp.where(
        (lax.broadcasted_iota(jnp.int32, (32, 128), 1) & 31) == lax.broadcasted_iota(jnp.int32, (32, 128), 0), 1.0, 0.0
    ).astype(BF16)
    sv = dot(sw[...].reshape(256, 32), rep4)
    zlane = lax.broadcasted_iota(jnp.int32, (32, 128), 1) // 32
    for m in range(4):
        wr = sv[m * 64 : m * 64 + 32]
        wi = sv[m * 64 + 32 : m * 64 + 64]
        for r in range(2):
            for z in range(4):
                first = jnp.where(zlane == z, wr if r == 0 else -wi, 0.0)
                second = jnp.where(zlane == z, wi if r == 0 else wr, 0.0)
                rmat[m, r * 128 + z * 32 : r * 128 + z * 32 + 32, :] = jnp.concatenate([first, second], axis=1).astype(BF16)

    load_w.wait()
    rep8 = jnp.where(
        (lax.broadcasted_iota(jnp.int32, (32, 256), 1) & 31) == lax.broadcasted_iota(jnp.int32, (32, 256), 0), 1.0, 0.0
    ).astype(BF16)
    wrep[...] = dot(cw[...].reshape(864, 32), rep8)
    zlane8 = lax.broadcasted_iota(jnp.int32, (32, 256), 1) // 32
    cmat[...] = jnp.zeros_like(cmat)

    def band(t, carry):
        dyi, dxi = t // 3, t % 3
        base = pl.multiple_of((dxi * 3 + dyi) * 96, 32)
        w = [wrep[pl.ds(pl.multiple_of(base + 32 * k, 32), 32), :] for k in range(3)]
        for z in range(8):
            block = jnp.where(zlane8 == z + 1, w[0], 0.0)
            block = jnp.where(zlane8 == z, w[1], block)
            block = jnp.where(zlane8 == z - 1, w[2], block)
            tmat[pl.ds(pl.multiple_of(t * 256 + z * 32, 32), 32), :] = block.astype(BF16)
        cmat[pl.ds(pl.multiple_of(t * 256 + 96, 32), 32), :] = jnp.where(zlane8 == 4, w[0], 0.0).astype(BF16)
        cmat[pl.ds(pl.multiple_of(t * 256 + 128, 32), 32), :] = jnp.where(zlane8 == 3, w[2], 0.0).astype(BF16)
        return carry

    lax.fori_loop(0, 9, band, 0)

    r_copies = []
    for ch in range(nch):
        c_copies[ch].wait_recv()
        total = part[ch, own_rows, :] + cland[ch].astype(F32)
        part[ch, own_rows, :] = total
        sbuf[ch] = total.astype(BF16)
        for j in range(1, ny):
            target = lax.rem(yc + j, ny)
            copy = remote(
                sbuf.at[ch, pl.ds(pl.multiple_of(target * 64, 64), 64)], rland.at[ch, j - 1],
                r_send.at[ch, j - 1], r_recv.at[ch, j - 1], ychip(j),
            )
            copy.start()
            r_copies.append(copy)

    def shift(first, count):
        cells = fs[1, pl.ds(first, count)].astype(F32)
        sub = lax.broadcasted_iota(jnp.int32, cells.shape, 1)
        fs[0, pl.ds(first, count)] = jnp.where(sub == 0, 0.0, pltpu.roll(cells, 1, 1)).astype(BF16)
        fs[2, pl.ds(first, count)] = jnp.where(sub == 7, 0.0, pltpu.roll(cells, 7, 1)).astype(BF16)

    def shift_block(b, carry):
        shift(1 + b * 32, 32)
        return carry

    lax.fori_loop(0, 4, shift_block, 0)
    for copy in x_copies:
        copy.wait()
    has_left = jnp.where(g > 0, 1.0, 0.0)
    has_right = jnp.where(g < ng - 1, 1.0, 0.0)
    k_copies = [
        remote(xland, cornl.at[0], k_send.at[0], k_recv.at[0], (g, nxt)),
        remote(xland, cornl.at[1], k_send.at[1], k_recv.at[1], (g, prev)),
    ]
    for copy in k_copies:
        copy.start()
    fs[1, 0:1] = (xland[0, 1:2].astype(F32) * has_left).astype(BF16)
    fs[1, 129:130] = (xland[1, 0:1].astype(F32) * has_right).astype(BF16)
    shift(0, 1)
    shift(129, 1)

    load_b.wait()
    bias_row = jnp.concatenate([bv[...]] * 16, axis=1)

    def windows(taps, first, count):
        low = jnp.concatenate([t[:, :256] for t in taps], axis=1)
        high = jnp.concatenate([t[:, 256:] for t in taps], axis=1)
        mid = jnp.concatenate([t[:, 128:384] for t in taps], axis=1)
        rows = low.shape[0]
        main = dot(jnp.concatenate([low, high], axis=0), tmat[first : first + count, :])
        cross = dot(mid, cmat[first : first + count, :])
        return jnp.concatenate(
            [
                main[:rows, :128], main[:rows, 128:] + cross[:, :128],
                main[rows:, :128] + cross[:, 128:], main[rows:, 128:],
            ],
            axis=1,
        )

    def conv_block(b, carry):
        taps = [fs[dy, pl.ds(b * 32 + dx, 32)].reshape(256, 512) for dy in range(3) for dx in range(3)]
        value = windows(taps, 0, 2304) + bias_row
        for t in range(4):
            conv[t, pl.ds(pl.multiple_of(b * 256, 256), 256), :] = value[:, 128 * t : 128 * t + 128]
        return carry

    lax.fori_loop(0, 2, conv_block, 0)

    a_copies = []
    f_copies = []
    own_piece = pl.ds(pl.multiple_of(core * 256 + yc * 64, 64), 64)
    mix_rows = pl.ds(pl.multiple_of(q * 64, 64), 64)
    for ch in range(nch):
        coef = part[ch, own_piece, :]
        for j in range(1, ny):
            r_copies[ch * (ny - 1) + j - 1].wait_recv()
            coef = coef + rland[ch, j - 1].astype(F32)
        pieces = []
        for m in range(4):
            rows = jnp.concatenate(
                [
                    jnp.concatenate(
                        [coef[m * 16 + 8 * r : m * 16 + 8 * r + 8, 128 * t : 128 * t + 128] for r in range(2)], axis=1
                    )
                    for t in range(tiles)
                ],
                axis=0,
            ).astype(BF16)
            mix = dot(rows, rmat[m])
            for r in range(2):
                pieces.append(
                    jnp.concatenate([mix[8 * t : 8 * t + 8, 128 * r : 128 * r + 128] for t in range(tiles)], axis=1)
                )
        mixed[ch, mix_rows, :] = jnp.concatenate(pieces, axis=0).astype(BF16)
        block = mixed.at[ch, mix_rows]
        for j in range(1, ny):
            copy = remote(block, block, a_send.at[ch, j - 1], a_recv.at[ch, j - 1], ychip(j))
            copy.start()
            a_copies.append(copy)
        copy = remote(block, block, f_send.at[ch, 0], f_recv.at[ch, 0], sib)
        copy.start()
        f_copies.append(copy)

    lax.fori_loop(2, 4, conv_block, 0)

    row = lax.broadcasted_iota(jnp.int32, (256, 160), 0)
    col = lax.broadcasted_iota(jnp.int32, (256, 160), 1)
    x = row & 127
    for copy in y_copies + k_copies:
        copy.wait()
    for side in range(2):
        yrow = 7 if side == 0 else 0
        inside = jnp.where(row < 128, x - 1, x + 1)
        picks = jnp.where((col == inside) & (col < 128), 1.0, 0.0)
        picks = jnp.where((row == 0) & (col == 128 + 8 + yrow), has_left, picks)
        picks = jnp.where((row == 255) & (col == 128 + 16 + yrow), has_right, picks)
        mid_rows = yland[side]
        source = jnp.concatenate([mid_rows, cornl[side].reshape(32, 512)], axis=0)
        moved = dot(picks.astype(BF16), source).astype(BF16)
        value = windows([moved[:128], mid_rows, moved[128:]], 1536 * side, 768)
        there = (h > 0) if side == 0 else (h < nh - 1)
        value = value * jnp.where(there, 1.0, 0.0)
        edge = pl.ds(0 if side == 0 else 7, 128, stride=8)
        for t in range(4):
            conv[t, edge, :] = conv[t, edge, :] + value[:, 128 * t : 128 * t + 128]

    load_i.wait()
    spread(iexp, gmat)

    for ch in range(nch):
        for j in range(1, ny):
            a_copies[ch * (ny - 1) + j - 1].wait_recv()
            source = core * ny + lax.rem(yc + ny - j, ny)
            block = mixed.at[ch, pl.ds(pl.multiple_of(source * 64, 64), 64)]
            copy = remote(block, block, f_send.at[ch, j], f_recv.at[ch, j], sib)
            copy.start()
            f_copies.append(copy)

    for ch in range(nch):
        for j in range(ny):
            f_copies[ch if j == 0 else nch + ch * (ny - 1) + j - 1].wait_recv()

        def finish(b, carry):
            rows = pl.ds(pl.multiple_of(b * 256, 256), 256)
            lanes = slice(ch * lc, (ch + 1) * lc)
            base = jnp.concatenate([conv[ch * tiles + t, rows, :] for t in range(tiles)], axis=1)
            value = dot(gmat[rows, :], mixed[ch]) + base
            value = 0.5 * value * (1.0 + lax.erf(value * (0.5**0.5)))
            out[pl.ds(b * 32, 32), :, lanes] = value.reshape(32, 8, lc).astype(BF16)
            return carry

        lax.fori_loop(0, 4, finish, 0)

    for copy in c_copies + r_copies + a_copies + f_copies:
        copy.wait_send()


def shards(field, conv_weight, conv_bias, spectral_weight):
    cells_x, cells_y, width = field.shape
    groups = lax.axis_size("gx")
    modes = spectral_weight.shape[0]
    ny = groups // 2
    lc = width // CHUNKS
    ftab, itab = expanded_tables(cells_x * groups, modes, groups, cells_y)
    dma = pltpu.SemaphoreType.DMA
    vmem = pltpu.VMEM
    scratch = [
        vmem((3, cells_x + 2, cells_y, width), BF16),
        vmem((64, 1024), BF16),
        vmem((128, 512), BF16),
        vmem((27, 32, 32), BF16),
        vmem((4, 2, 32, 32), BF16),
        vmem((1, 32), F32),
        vmem((512, 1024), BF16),
        vmem((1024, 512), BF16),
        vmem((864, 256), F32),
        vmem((2304, 256), BF16),
        vmem((2304, 256), BF16),
        vmem((4, 256, 256), BF16),
        vmem((4, 1024, 128), F32),
        vmem((CHUNKS, 512, lc), F32),
        vmem((CHUNKS, 256, lc), BF16),
        vmem((CHUNKS, 256, lc), BF16),
        vmem((CHUNKS, 256, lc), BF16),
        vmem((CHUNKS, ny - 1, 64, lc), BF16),
        vmem((CHUNKS, 512, lc), BF16),
        vmem((2, 128, 512), BF16),
        vmem((2, 128, 512), BF16),
        vmem((2, 2, 8, 512), BF16),
        vmem((2, 2, 2, 8, 512), BF16),
        dma((6,)), dma((1,)),
        dma((CHUNKS,)), dma((CHUNKS,)),
        dma((CHUNKS, ny - 1)), dma((CHUNKS, ny - 1)),
        dma((CHUNKS, ny - 1)), dma((CHUNKS, ny - 1)),
        dma((CHUNKS, ny)), dma((CHUNKS, ny)),
        dma((2,)), dma((2,)), dma((2,)), dma((2,)), dma((2,)), dma((2,)),
    ]
    anywhere = pl.BlockSpec(memory_space=pl.ANY)
    return pl.pallas_call(
        layer_kernel,
        out_shape=jax.ShapeDtypeStruct(field.shape, BF16),
        in_specs=[anywhere] * 6,
        out_specs=pl.BlockSpec(memory_space=pltpu.VMEM),
        scratch_shapes=scratch,
        compiler_params=pltpu.CompilerParams(
            collective_id=0, has_side_effects=True, vmem_limit_bytes=40 * 1024 * 1024
        ),
        name="layer",
    )(field, conv_weight, conv_bias.reshape(1, -1), spectral_weight, ftab, itab)


def solution(mesh):
    placed = (P("gx", "gy", None), P(), P(), P())
    return jax.shard_map(
        shards, mesh=mesh, in_specs=placed, out_specs=P("gx", "gy", None), check_vma=False
    )
```

```python
import functools
import math

import jax
import jax.numpy as jnp
import numpy as np
from jax import lax
from jax.experimental import pallas as pl
from jax.experimental.pallas import tpu as pltpu
from jax.sharding import PartitionSpec as P

MESH = pl.DeviceIdType.MESH
CHUNKS = 2
F32 = jnp.float32
BF16 = jnp.bfloat16


def dot(a, b):
    return jnp.dot(a, b, preferred_element_type=F32)


def expanded_tables(length, modes, groups, rows_y):
    turns = (np.arange(modes)[:, None] * np.arange(length)[None, :]) % length
    angles = turns.astype(np.float32) * np.float32(2.0 * math.pi / length)
    pairs = np.stack([np.cos(angles), -np.sin(angles)], axis=1) * np.float32(1.0 / math.sqrt(length))
    doubling = np.where(np.arange(modes) == 0, 1.0, 2.0).astype(np.float32)
    forward = pairs.reshape(2 * modes, groups, length // groups).transpose(1, 0, 2)
    inverse = (pairs * doubling[:, None, None]).reshape(2 * modes, groups, length // groups).transpose(1, 2, 0)
    forward = np.repeat(forward, rows_y, axis=2)
    inverse = np.repeat(inverse, rows_y, axis=2)
    return jnp.asarray(forward, BF16), jnp.asarray(inverse, BF16)


def spread(table_ref, out_ref):
    rows, lanes = table_ref.shape

    def body(i, carry):
        part = table_ref[pl.ds(pl.multiple_of(i * 16, 16), 16), :].astype(F32)
        wide = jnp.broadcast_to(part[:, None, :], (16, 8, lanes))
        keep = lax.broadcasted_iota(jnp.int32, (16, 8, lanes), 1) == (
            lax.broadcasted_iota(jnp.int32, (16, 8, lanes), 2) & 7
        )
        out_ref[pl.ds(pl.multiple_of(i * 128, 128), 128), :] = (
            jnp.where(keep, wide, 0.0).reshape(128, lanes).astype(BF16)
        )
        return carry

    lax.fori_loop(0, rows // 16, body, 0)


def layer_kernel(
    field, convw, bias, specw, ftab, itab, out,
    fs, fexp, iexp, cw, sw, bv, amat, gmat, wrep, tmat, cmat, rmat, conv,
    part, cbuf, cland, sbuf, rland, mixed, ybuf, yland, xland, cornl,
    load_sem, bar_send, c_send, c_recv, r_send, r_recv, a_send, a_recv, f_send, f_recv,
    x_send, x_recv, y_send, y_recv, k_send, k_recv,
):
    nch, _, lc = mixed.shape
    tiles = lc // 128
    g = lax.axis_index("gx")
    h = lax.axis_index("gy")
    ng = lax.axis_size("gx")
    nh = lax.axis_size("gy")
    ny = ng // 2
    yc, core = g // 2, g % 2
    q = core * ny + yc
    sib = (2 * yc + (1 - core), h)

    def ychip(j):
        return (2 * lax.rem(yc + j, ny) + core, h)

    left, right = lax.rem(g + ng - 1, ng), lax.rem(g + 1, ng)
    prev, nxt = lax.rem(h + nh - 1, nh), lax.rem(h + 1, nh)
    outer = lax.rem(g + ng + 2 * core - 1, ng)

    def remote(src, dst, s, r, dev):
        return pltpu.make_async_remote_copy(
            src_ref=src, dst_ref=dst, send_sem=s, recv_sem=r, device_id=dev, device_id_type=MESH
        )

    barrier = pltpu.get_barrier_semaphore()
    partners = [sib] + [ychip(j) for j in range(1, ny)] + [(outer, h), (g, prev), (g, nxt)]
    for dev in partners:
        pl.semaphore_signal(barrier, inc=1, device_id=dev, device_id_type=MESH)

    load_f = pltpu.make_async_copy(ftab.at[g], fexp, load_sem.at[0])
    load_x = pltpu.make_async_copy(field, fs.at[1, pl.ds(1, 128)], load_sem.at[1])
    load_i = pltpu.make_async_copy(itab.at[g], iexp, load_sem.at[2])
    load_w = pltpu.make_async_copy(convw, cw, load_sem.at[3])
    load_s = pltpu.make_async_copy(specw.at[pl.ds(4 * q, 4)], sw, load_sem.at[4])
    load_b = pltpu.make_async_copy(bias, bv, load_sem.at[5])
    for load in (load_f, load_x, load_w, load_s, load_i, load_b):
        load.start()

    load_f.wait()
    spread(fexp, amat)
    load_x.wait()
    pl.semaphore_wait(barrier, len(partners))
    x_copies = [
        remote(fs.at[1, pl.ds(127, 2)], xland.at[0], x_send.at[0], x_recv.at[0], (right, h)),
        remote(fs.at[1, pl.ds(1, 2)], xland.at[1], x_send.at[1], x_recv.at[1], (left, h)),
    ]
    for copy in x_copies:
        copy.start()
    c_copies = []
    own_rows = pl.ds(pl.multiple_of(core * 256, 256), 256)
    sib_rows = pl.ds(pl.multiple_of((1 - core) * 256, 256), 256)
    for ch in range(nch):
        cells = fs[1, 1:129, :, ch * lc : (ch + 1) * lc].reshape(1024, lc)
        part[ch] = dot(amat[...], cells)
        cbuf[ch] = part[ch, sib_rows, :].astype(BF16)
        copy = remote(cbuf.at[ch], cland.at[ch], c_send.at[ch], c_recv.at[ch], sib)
        copy.start()
        c_copies.append(copy)

    row = lax.broadcasted_iota(jnp.int32, (64, 256), 0)
    col = lax.broadcasted_iota(jnp.int32, (64, 256), 1)
    pick = jnp.where(col == (row & 31) * 8 + jnp.where(row < 32, 7, 0), 1.0, 0.0).astype(BF16)
    for b in range(4):
        cells = fs[1, 1 + 32 * b : 33 + 32 * b].reshape(256, 512)
        picked = dot(pick, cells).astype(BF16)
        ybuf[0, 32 * b : 32 * b + 32, :] = picked[:32]
        ybuf[1, 32 * b : 32 * b + 32, :] = picked[32:]
    y_copies = [
        remote(ybuf.at[0], yland.at[0], y_send.at[0], y_recv.at[0], (g, nxt)),
        remote(ybuf.at[1], yland.at[1], y_send.at[1], y_recv.at[1], (g, prev)),
    ]
    for copy in y_copies:
        copy.start()

    load_s.wait()
    rep4 = jnp.where(
        (lax.broadcasted_iota(jnp.int32, (32, 128), 1) & 31) == lax.broadcasted_iota(jnp.int32, (32, 128), 0), 1.0, 0.0
    ).astype(BF16)
    sv = dot(sw[...].reshape(256, 32), rep4)
    zlane = lax.broadcasted_iota(jnp.int32, (32, 128), 1) // 32
    for m in range(4):
        wr = sv[m * 64 : m * 64 + 32]
        wi = sv[m * 64 + 32 : m * 64 + 64]
        for r in range(2):
            for z in range(4):
                first = jnp.where(zlane == z, wr if r == 0 else -wi, 0.0)
                second = jnp.where(zlane == z, wi if r == 0 else wr, 0.0)
                rmat[m, r * 128 + z * 32 : r * 128 + z * 32 + 32, :] = jnp.concatenate([first, second], axis=1).astype(BF16)

    load_w.wait()
    rep8 = jnp.where(
        (lax.broadcasted_iota(jnp.int32, (32, 256), 1) & 31) == lax.broadcasted_iota(jnp.int32, (32, 256), 0), 1.0, 0.0
    ).astype(BF16)
    wrep[...] = dot(cw[...].reshape(864, 32), rep8)
    zlane8 = lax.broadcasted_iota(jnp.int32, (32, 256), 1) // 32
    cmat[...] = jnp.zeros_like(cmat)

    def band(t, carry):
        dyi, dxi = t // 3, t % 3
        base = pl.multiple_of((dxi * 3 + dyi) * 96, 32)
        w = [wrep[pl.ds(pl.multiple_of(base + 32 * k, 32), 32), :] for k in range(3)]
        for z in range(8):
            block = jnp.where(zlane8 == z + 1, w[0], 0.0)
            block = jnp.where(zlane8 == z, w[1], block)
            block = jnp.where(zlane8 == z - 1, w[2], block)
            tmat[pl.ds(pl.multiple_of(t * 256 + z * 32, 32), 32), :] = block.astype(BF16)
        cmat[pl.ds(pl.multiple_of(t * 256 + 96, 32), 32), :] = jnp.where(zlane8 == 4, w[0], 0.0).astype(BF16)
        cmat[pl.ds(pl.multiple_of(t * 256 + 128, 32), 32), :] = jnp.where(zlane8 == 3, w[2], 0.0).astype(BF16)
        return carry

    lax.fori_loop(0, 9, band, 0)

    r_copies = []
    for ch in range(nch):
        c_copies[ch].wait_recv()
        total = part[ch, own_rows, :] + cland[ch].astype(F32)
        part[ch, own_rows, :] = total
        sbuf[ch] = total.astype(BF16)
        for j in range(1, ny):
            target = lax.rem(yc + j, ny)
            copy = remote(
                sbuf.at[ch, pl.ds(pl.multiple_of(target * 64, 64), 64)], rland.at[ch, j - 1],
                r_send.at[ch, j - 1], r_recv.at[ch, j - 1], ychip(j),
            )
            copy.start()
            r_copies.append(copy)

    def shift(first, count):
        cells = fs[1, pl.ds(first, count)].astype(F32)
        sub = lax.broadcasted_iota(jnp.int32, cells.shape, 1)
        fs[0, pl.ds(first, count)] = jnp.where(sub == 0, 0.0, pltpu.roll(cells, 1, 1)).astype(BF16)
        fs[2, pl.ds(first, count)] = jnp.where(sub == 7, 0.0, pltpu.roll(cells, 7, 1)).astype(BF16)

    def shift_block(b, carry):
        shift(1 + b * 32, 32)
        return carry

    lax.fori_loop(0, 4, shift_block, 0)
    for copy in x_copies:
        copy.wait()
    has_left = jnp.where(g > 0, 1.0, 0.0)
    has_right = jnp.where(g < ng - 1, 1.0, 0.0)
    k_copies = [
        remote(xland, cornl.at[0], k_send.at[0], k_recv.at[0], (g, nxt)),
        remote(xland, cornl.at[1], k_send.at[1], k_recv.at[1], (g, prev)),
    ]
    for copy in k_copies:
        copy.start()
    fs[1, 0:1] = (xland[0, 1:2].astype(F32) * has_left).astype(BF16)
    fs[1, 129:130] = (xland[1, 0:1].astype(F32) * has_right).astype(BF16)
    shift(0, 1)
    shift(129, 1)

    load_b.wait()
    bias_row = jnp.concatenate([bv[...]] * 16, axis=1)

    def windows(taps, first, count):
        low = jnp.concatenate([t[:, :256] for t in taps], axis=1)
        high = jnp.concatenate([t[:, 256:] for t in taps], axis=1)
        mid = jnp.concatenate([t[:, 128:384] for t in taps], axis=1)
        rows = low.shape[0]
        main = dot(jnp.concatenate([low, high], axis=0), tmat[first : first + count, :])
        cross = dot(mid, cmat[first : first + count, :])
        return jnp.concatenate(
            [
                main[:rows, :128], main[:rows, 128:] + cross[:, :128],
                main[rows:, :128] + cross[:, 128:], main[rows:, 128:],
            ],
            axis=1,
        )

    def conv_block(b, carry):
        taps = [fs[dy, pl.ds(b * 32 + dx, 32)].reshape(256, 512) for dy in range(3) for dx in range(3)]
        value = windows(taps, 0, 2304) + bias_row
        for t in range(4):
            conv[t, pl.ds(pl.multiple_of(b * 256, 256), 256), :] = value[:, 128 * t : 128 * t + 128]
        return carry

    lax.fori_loop(0, 2, conv_block, 0)

    a_copies = []
    f_copies = []
    own_piece = pl.ds(pl.multiple_of(core * 256 + yc * 64, 64), 64)
    mix_rows = pl.ds(pl.multiple_of(q * 64, 64), 64)
    for ch in range(nch):
        coef = part[ch, own_piece, :]
        for j in range(1, ny):
            r_copies[ch * (ny - 1) + j - 1].wait_recv()
            coef = coef + rland[ch, j - 1].astype(F32)
        pieces = []
        for m in range(4):
            rows = jnp.concatenate(
                [
                    jnp.concatenate(
                        [coef[m * 16 + 8 * r : m * 16 + 8 * r + 8, 128 * t : 128 * t + 128] for r in range(2)], axis=1
                    )
                    for t in range(tiles)
                ],
                axis=0,
            ).astype(BF16)
            mix = dot(rows, rmat[m])
            for r in range(2):
                pieces.append(
                    jnp.concatenate([mix[8 * t : 8 * t + 8, 128 * r : 128 * r + 128] for t in range(tiles)], axis=1)
                )
        mixed[ch, mix_rows, :] = jnp.concatenate(pieces, axis=0).astype(BF16)
        block = mixed.at[ch, mix_rows]
        for j in range(1, ny):
            copy = remote(block, block, a_send.at[ch, j - 1], a_recv.at[ch, j - 1], ychip(j))
            copy.start()
            a_copies.append(copy)
        copy = remote(block, block, f_send.at[ch, 0], f_recv.at[ch, 0], sib)
        copy.start()
        f_copies.append(copy)

    lax.fori_loop(2, 4, conv_block, 0)

    row = lax.broadcasted_iota(jnp.int32, (256, 160), 0)
    col = lax.broadcasted_iota(jnp.int32, (256, 160), 1)
    x = row & 127
    for copy in y_copies + k_copies:
        copy.wait()
    for side in range(2):
        yrow = 7 if side == 0 else 0
        inside = jnp.where(row < 128, x - 1, x + 1)
        picks = jnp.where((col == inside) & (col < 128), 1.0, 0.0)
        picks = jnp.where((row == 0) & (col == 128 + 8 + yrow), has_left, picks)
        picks = jnp.where((row == 255) & (col == 128 + 16 + yrow), has_right, picks)
        mid_rows = yland[side]
        source = jnp.concatenate([mid_rows, cornl[side].reshape(32, 512)], axis=0)
        moved = dot(picks.astype(BF16), source).astype(BF16)
        value = windows([moved[:128], mid_rows, moved[128:]], 1536 * side, 768)
        there = (h > 0) if side == 0 else (h < nh - 1)
        value = value * jnp.where(there, 1.0, 0.0)
        edge = pl.ds(0 if side == 0 else 7, 128, stride=8)
        for t in range(4):
            conv[t, edge, :] = conv[t, edge, :] + value[:, 128 * t : 128 * t + 128]

    load_i.wait()
    spread(iexp, gmat)

    for ch in range(nch):
        for j in range(1, ny):
            a_copies[ch * (ny - 1) + j - 1].wait_recv()
            source = core * ny + lax.rem(yc + ny - j, ny)
            block = mixed.at[ch, pl.ds(pl.multiple_of(source * 64, 64), 64)]
            copy = remote(block, block, f_send.at[ch, j], f_recv.at[ch, j], sib)
            copy.start()
            f_copies.append(copy)

    for ch in range(nch):
        for j in range(ny):
            f_copies[ch if j == 0 else nch + ch * (ny - 1) + j - 1].wait_recv()

        def finish(b, carry):
            rows = pl.ds(pl.multiple_of(b * 256, 256), 256)
            lanes = slice(ch * lc, (ch + 1) * lc)
            base = jnp.concatenate([conv[ch * tiles + t, rows, :] for t in range(tiles)], axis=1)
            value = dot(gmat[rows, :], mixed[ch]) + base
            value = 0.5 * value * (1.0 + lax.erf(value * (0.5**0.5)))
            out[pl.ds(b * 32, 32), :, lanes] = value.reshape(32, 8, lc).astype(BF16)
            return carry

        lax.fori_loop(0, 4, finish, 0)

    for copy in c_copies + r_copies + a_copies + f_copies:
        copy.wait_send()


def shards(field, conv_weight, conv_bias, spectral_weight):
    cells_x, cells_y, width = field.shape
    groups = lax.axis_size("gx")
    modes = spectral_weight.shape[0]
    ny = groups // 2
    lc = width // CHUNKS
    ftab, itab = expanded_tables(cells_x * groups, modes, groups, cells_y)
    dma = pltpu.SemaphoreType.DMA
    vmem = pltpu.VMEM
    scratch = [
        vmem((3, cells_x + 2, cells_y, width), BF16),
        vmem((64, 1024), BF16),
        vmem((128, 512), BF16),
        vmem((27, 32, 32), BF16),
        vmem((4, 2, 32, 32), BF16),
        vmem((1, 32), F32),
        vmem((512, 1024), BF16),
        vmem((1024, 512), BF16),
        vmem((864, 256), F32),
        vmem((2304, 256), BF16),
        vmem((2304, 256), BF16),
        vmem((4, 256, 256), BF16),
        vmem((4, 1024, 128), F32),
        vmem((CHUNKS, 512, lc), F32),
        vmem((CHUNKS, 256, lc), BF16),
        vmem((CHUNKS, 256, lc), BF16),
        vmem((CHUNKS, 256, lc), BF16),
        vmem((CHUNKS, ny - 1, 64, lc), BF16),
        vmem((CHUNKS, 512, lc), BF16),
        vmem((2, 128, 512), BF16),
        vmem((2, 128, 512), BF16),
        vmem((2, 2, 8, 512), BF16),
        vmem((2, 2, 2, 8, 512), BF16),
        dma((6,)), dma((1,)),
        dma((CHUNKS,)), dma((CHUNKS,)),
        dma((CHUNKS, ny - 1)), dma((CHUNKS, ny - 1)),
        dma((CHUNKS, ny - 1)), dma((CHUNKS, ny - 1)),
        dma((CHUNKS, ny)), dma((CHUNKS, ny)),
        dma((2,)), dma((2,)), dma((2,)), dma((2,)), dma((2,)), dma((2,)),
    ]
    operands = (field, conv_weight, conv_bias.reshape(1, -1), spectral_weight, ftab, itab)
    in_hbm = pl.BlockSpec(memory_space=pltpu.HBM)
    return pl.pallas_call(
        layer_kernel,
        out_shape=jax.ShapeDtypeStruct(field.shape, BF16),
        in_specs=[in_hbm] * 6,
        out_specs=pl.BlockSpec(memory_space=pltpu.VMEM),
        scratch_shapes=scratch,
        compiler_params=pltpu.CompilerParams(
            collective_id=0, has_side_effects=True, vmem_limit_bytes=40 * 1024 * 1024
        ),
        name="layer",
    )(*(pltpu.with_memory_space_constraint(a, pltpu.HBM) for a in operands))


def solution(mesh):
    placed = (P("gx", "gy", None), P(), P(), P())
    return jax.shard_map(
        shards, mesh=mesh, in_specs=placed, out_specs=P("gx", "gy", None), check_vma=False
    )
```

```python
import functools
import math

import jax
import jax.numpy as jnp
import numpy as np
from jax import lax
from jax.experimental import pallas as pl
from jax.experimental.pallas import tpu as pltpu
from jax.sharding import PartitionSpec as P

MESH = pl.DeviceIdType.MESH
CHUNKS = 2
F32 = jnp.float32
BF16 = jnp.bfloat16


def dot(a, b):
    return jnp.dot(a, b, preferred_element_type=F32)


def expanded_tables(length, modes, groups, rows_y):
    turns = (np.arange(modes)[:, None] * np.arange(length)[None, :]) % length
    angles = turns.astype(np.float32) * np.float32(2.0 * math.pi / length)
    pairs = np.stack([np.cos(angles), -np.sin(angles)], axis=1) * np.float32(1.0 / math.sqrt(length))
    doubling = np.where(np.arange(modes) == 0, 1.0, 2.0).astype(np.float32)
    forward = pairs.reshape(2 * modes, groups, length // groups).transpose(1, 0, 2)
    inverse = (pairs * doubling[:, None, None]).reshape(2 * modes, groups, length // groups).transpose(1, 2, 0)
    forward = np.repeat(forward, rows_y, axis=2)
    inverse = np.kron(inverse, np.eye(rows_y, dtype=np.float32))
    return jnp.asarray(forward, BF16), jnp.asarray(inverse, BF16)


def spread(table_ref, out_ref):
    rows, lanes = table_ref.shape

    def body(i, carry):
        part = table_ref[pl.ds(pl.multiple_of(i * 16, 16), 16), :].astype(F32)
        wide = jnp.broadcast_to(part[:, None, :], (16, 8, lanes))
        keep = lax.broadcasted_iota(jnp.int32, (16, 8, lanes), 1) == (
            lax.broadcasted_iota(jnp.int32, (16, 8, lanes), 2) & 7
        )
        out_ref[pl.ds(pl.multiple_of(i * 128, 128), 128), :] = (
            jnp.where(keep, wide, 0.0).reshape(128, lanes).astype(BF16)
        )
        return carry

    lax.fori_loop(0, rows // 16, body, 0)


def layer_kernel(
    field, convw, bias, specw, ftab, itab, out,
    fs, fexp, cw, sw, bv, amat, gmat, wrep, tmat, cmat, rmat, conv,
    part, cbuf, cland, sbuf, rland, mixed, ybuf, yland, xland, cornl,
    load_sem, bar_send, c_send, c_recv, r_send, r_recv, a_send, a_recv, f_send, f_recv,
    x_send, x_recv, y_send, y_recv, k_send, k_recv, ready,
):
    nch, _, lc = mixed.shape
    tiles = lc // 128
    g = lax.axis_index("gx")
    h = lax.axis_index("gy")
    ng = lax.axis_size("gx")
    nh = lax.axis_size("gy")
    ny = ng // 2
    yc, core = g // 2, g % 2
    q = core * ny + yc
    sib = (2 * yc + (1 - core), h)

    def ychip(j):
        return (2 * lax.rem(yc + j, ny) + core, h)

    left, right = lax.rem(g + ng - 1, ng), lax.rem(g + 1, ng)
    prev, nxt = lax.rem(h + nh - 1, nh), lax.rem(h + 1, nh)
    outer = lax.rem(g + ng + 2 * core - 1, ng)

    def remote(src, dst, s, r, dev):
        return pltpu.make_async_remote_copy(
            src_ref=src, dst_ref=dst, send_sem=s, recv_sem=r, device_id=dev, device_id_type=MESH
        )

    barrier = pltpu.get_barrier_semaphore()
    partners = [sib] + [ychip(j) for j in range(1, ny)] + [(outer, h)]
    for dev in partners:
        pl.semaphore_signal(barrier, inc=1, device_id=dev, device_id_type=MESH)
    first_up = lax.rem(h + 1, 8) != 0
    first_down = lax.rem(h, 8) == 0
    has_up, has_down = h < nh - 1, h > 0
    pairs = [
        (has_down, first_down, (g, prev), 1),
        (has_up, first_up, (g, nxt), 0),
    ]
    waits = jnp.int32(len(partners))
    for there, first, dev, _ in pairs:

        @pl.when(there & first)
        def _(dev=dev):
            pl.semaphore_signal(barrier, inc=1, device_id=dev, device_id_type=MESH)

        waits = waits + jnp.where(there & ~first, 1, 0)

    load_f = pltpu.make_async_copy(ftab.at[g], fexp, load_sem.at[0])
    load_x = pltpu.make_async_copy(field, fs.at[1, pl.ds(1, 128)], load_sem.at[1])
    load_i = pltpu.make_async_copy(itab.at[g], gmat, load_sem.at[2])
    load_w = pltpu.make_async_copy(convw, cw, load_sem.at[3])
    load_s = pltpu.make_async_copy(specw.at[pl.ds(4 * q, 4)], sw, load_sem.at[4])
    load_b = pltpu.make_async_copy(bias, bv, load_sem.at[5])
    for load in (load_f, load_w, load_s, load_x, load_b, load_i):
        load.start()

    load_f.wait()
    spread(fexp, amat)
    load_s.wait()
    rep4 = jnp.where(
        (lax.broadcasted_iota(jnp.int32, (32, 128), 1) & 31) == lax.broadcasted_iota(jnp.int32, (32, 128), 0), 1.0, 0.0
    ).astype(BF16)
    sv = dot(sw[...].reshape(256, 32), rep4)
    zlane = lax.broadcasted_iota(jnp.int32, (32, 128), 1) // 32
    for m in range(4):
        wr = sv[m * 64 : m * 64 + 32]
        wi = sv[m * 64 + 32 : m * 64 + 64]
        for r in range(2):
            for z in range(4):
                first = jnp.where(zlane == z, wr if r == 0 else -wi, 0.0)
                second = jnp.where(zlane == z, wi if r == 0 else wr, 0.0)
                rmat[m, r * 128 + z * 32 : r * 128 + z * 32 + 32, :] = jnp.concatenate([first, second], axis=1).astype(BF16)

    load_w.wait()
    rep8 = jnp.where(
        (lax.broadcasted_iota(jnp.int32, (32, 256), 1) & 31) == lax.broadcasted_iota(jnp.int32, (32, 256), 0), 1.0, 0.0
    ).astype(BF16)
    wrep[...] = dot(cw[...].reshape(864, 32), rep8)
    zlane8 = lax.broadcasted_iota(jnp.int32, (32, 256), 1) // 32
    cmat[...] = jnp.zeros_like(cmat)

    def band(t, carry):
        dyi, dxi = t // 3, t % 3
        base = pl.multiple_of((dxi * 3 + dyi) * 96, 32)
        w = [wrep[pl.ds(pl.multiple_of(base + 32 * k, 32), 32), :] for k in range(3)]
        for z in range(8):
            block = jnp.where(zlane8 == z + 1, w[0], 0.0)
            block = jnp.where(zlane8 == z, w[1], block)
            block = jnp.where(zlane8 == z - 1, w[2], block)
            tmat[pl.ds(pl.multiple_of(t * 256 + z * 32, 32), 32), :] = block.astype(BF16)
        cmat[pl.ds(pl.multiple_of(t * 256 + 96, 32), 32), :] = jnp.where(zlane8 == 4, w[0], 0.0).astype(BF16)
        cmat[pl.ds(pl.multiple_of(t * 256 + 128, 32), 32), :] = jnp.where(zlane8 == 3, w[2], 0.0).astype(BF16)
        return carry

    lax.fori_loop(0, 4, band, 0)
    load_x.wait()
    pl.semaphore_wait(barrier, waits)
    for there, first, dev, lands in pairs:

        @pl.when(there & ~first)
        def _(dev=dev, lands=lands):
            pl.semaphore_signal(ready.at[lands], inc=1, device_id=dev, device_id_type=MESH)

    x_copies = [
        remote(fs.at[1, pl.ds(127, 2)], xland.at[0], x_send.at[0], x_recv.at[0], (right, h)),
        remote(fs.at[1, pl.ds(1, 2)], xland.at[1], x_send.at[1], x_recv.at[1], (left, h)),
    ]
    for copy in x_copies:
        copy.start()
    c_copies = []
    own_rows = pl.ds(pl.multiple_of(core * 256, 256), 256)
    sib_rows = pl.ds(pl.multiple_of((1 - core) * 256, 256), 256)
    for ch in range(nch):
        cells = fs[1, 1:129, :, ch * lc : (ch + 1) * lc].reshape(1024, lc)
        part[ch] = dot(amat[...], cells)
        cbuf[ch] = part[ch, sib_rows, :].astype(BF16)
        copy = remote(cbuf.at[ch], cland.at[ch], c_send.at[ch], c_recv.at[ch], sib)
        copy.start()
        c_copies.append(copy)

    row = lax.broadcasted_iota(jnp.int32, (64, 256), 0)
    col = lax.broadcasted_iota(jnp.int32, (64, 256), 1)
    pick = jnp.where(col == (row & 31) * 8 + jnp.where(row < 32, 7, 0), 1.0, 0.0).astype(BF16)
    for b in range(4):
        cells = fs[1, 1 + 32 * b : 33 + 32 * b].reshape(256, 512)
        picked = dot(pick, cells).astype(BF16)
        ybuf[0, 32 * b : 32 * b + 32, :] = picked[:32]
        ybuf[1, 32 * b : 32 * b + 32, :] = picked[32:]
    y_copies = [
        remote(ybuf.at[1], yland.at[1], y_send.at[1], y_recv.at[1], (g, prev)),
        remote(ybuf.at[0], yland.at[0], y_send.at[0], y_recv.at[0], (g, nxt)),
    ]
    k_copies = [
        remote(xland, cornl.at[1], k_send.at[1], k_recv.at[1], (g, prev)),
        remote(xland, cornl.at[0], k_send.at[0], k_recv.at[0], (g, nxt)),
    ]
    for (there, first, _, _), copy in zip(pairs, y_copies):
        pl.when(there & ~first)(copy.start)

    lax.fori_loop(4, 9, band, 0)

    r_copies = []
    for ch in range(nch):
        c_copies[ch].wait_recv()
        total = part[ch, own_rows, :] + cland[ch].astype(F32)
        part[ch, own_rows, :] = total
        sbuf[ch] = total.astype(BF16)
        for j in range(1, ny):
            target = lax.rem(yc + j, ny)
            copy = remote(
                sbuf.at[ch, pl.ds(pl.multiple_of(target * 64, 64), 64)], rland.at[ch, j - 1],
                r_send.at[ch, j - 1], r_recv.at[ch, j - 1], ychip(j),
            )
            copy.start()
            r_copies.append(copy)

    def shift(first, count):
        cells = fs[1, pl.ds(first, count)].astype(F32)
        sub = lax.broadcasted_iota(jnp.int32, cells.shape, 1)
        fs[0, pl.ds(first, count)] = jnp.where(sub == 0, 0.0, pltpu.roll(cells, 1, 1)).astype(BF16)
        fs[2, pl.ds(first, count)] = jnp.where(sub == 7, 0.0, pltpu.roll(cells, 7, 1)).astype(BF16)

    def shift_block(b, carry):
        shift(1 + b * 32, 32)
        return carry

    lax.fori_loop(0, 4, shift_block, 0)
    for copy in x_copies:
        copy.wait()
    has_left = jnp.where(g > 0, 1.0, 0.0)
    has_right = jnp.where(g < ng - 1, 1.0, 0.0)
    for (there, first, _, _), copy in zip(pairs, k_copies):
        pl.when(there & ~first)(copy.start)
    fs[1, 0:1] = (xland[0, 1:2].astype(F32) * has_left).astype(BF16)
    fs[1, 129:130] = (xland[1, 0:1].astype(F32) * has_right).astype(BF16)
    shift(0, 1)
    shift(129, 1)

    load_b.wait()
    bias_row = jnp.concatenate([bv[...]] * 16, axis=1)

    def windows(taps, first, count):
        low = jnp.concatenate([t[:, :256] for t in taps], axis=1)
        high = jnp.concatenate([t[:, 256:] for t in taps], axis=1)
        mid = jnp.concatenate([t[:, 128:384] for t in taps], axis=1)
        rows = low.shape[0]
        main = dot(jnp.concatenate([low, high], axis=0), tmat[first : first + count, :])
        cross = dot(mid, cmat[first : first + count, :])
        return jnp.concatenate(
            [
                main[:rows, :128], main[:rows, 128:] + cross[:, :128],
                main[rows:, :128] + cross[:, 128:], main[rows:, 128:],
            ],
            axis=1,
        )

    def conv_block(b, carry):
        taps = [fs[dy, pl.ds(b * 32 + dx, 32)].reshape(256, 512) for dy in range(3) for dx in range(3)]
        value = windows(taps, 0, 2304) + bias_row
        for t in range(4):
            conv[t, pl.ds(pl.multiple_of(b * 256, 256), 256), :] = value[:, 128 * t : 128 * t + 128]
        return carry

    lax.fori_loop(0, 2, conv_block, 0)

    a_copies = []
    f_copies = []
    own_piece = pl.ds(pl.multiple_of(core * 256 + yc * 64, 64), 64)
    mix_rows = pl.ds(pl.multiple_of(q * 64, 64), 64)
    for ch in range(nch):
        coef = part[ch, own_piece, :]
        for j in range(1, ny):
            r_copies[ch * (ny - 1) + j - 1].wait_recv()
            coef = coef + rland[ch, j - 1].astype(F32)
        pieces = []
        for m in range(4):
            rows = jnp.concatenate(
                [
                    jnp.concatenate(
                        [coef[m * 16 + 8 * r : m * 16 + 8 * r + 8, 128 * t : 128 * t + 128] for r in range(2)], axis=1
                    )
                    for t in range(tiles)
                ],
                axis=0,
            ).astype(BF16)
            mix = dot(rows, rmat[m])
            for r in range(2):
                pieces.append(
                    jnp.concatenate([mix[8 * t : 8 * t + 8, 128 * r : 128 * r + 128] for t in range(tiles)], axis=1)
                )
        mixed[ch, mix_rows, :] = jnp.concatenate(pieces, axis=0).astype(BF16)
        block = mixed.at[ch, mix_rows]
        for j in range(1, ny):
            copy = remote(block, block, a_send.at[ch, j - 1], a_recv.at[ch, j - 1], ychip(j))
            copy.start()
            a_copies.append(copy)
        copy = remote(block, block, f_send.at[ch, 0], f_recv.at[ch, 0], sib)
        copy.start()
        f_copies.append(copy)

    for (there, first, _, lands), y_copy, k_copy in zip(pairs, y_copies, k_copies):

        @pl.when(there & first)
        def _(lands=lands, y_copy=y_copy, k_copy=k_copy):
            pl.semaphore_wait(ready.at[1 - lands], 1)
            y_copy.start()
            k_copy.start()

    lax.fori_loop(2, 4, conv_block, 0)

    row = lax.broadcasted_iota(jnp.int32, (256, 160), 0)
    col = lax.broadcasted_iota(jnp.int32, (256, 160), 1)
    x = row & 127
    for side in range(2):

        @pl.when(pairs[side][0])
        def _(side=side):
            y_copies[1 - side].wait_recv()
            k_copies[1 - side].wait_recv()
            yrow = 7 if side == 0 else 0
            inside = jnp.where(row < 128, x - 1, x + 1)
            picks = jnp.where((col == inside) & (col < 128), 1.0, 0.0)
            picks = jnp.where((row == 0) & (col == 128 + 8 + yrow), has_left, picks)
            picks = jnp.where((row == 255) & (col == 128 + 16 + yrow), has_right, picks)
            mid_rows = yland[side]
            source = jnp.concatenate([mid_rows, cornl[side].reshape(32, 512)], axis=0)
            moved = dot(picks.astype(BF16), source).astype(BF16)
            value = windows([moved[:128], mid_rows, moved[128:]], 1536 * side, 768)
            edge = pl.ds(0 if side == 0 else 7, 128, stride=8)
            for t in range(4):
                conv[t, edge, :] = conv[t, edge, :] + value[:, 128 * t : 128 * t + 128]

    for ch in range(nch):
        for j in range(1, ny):
            a_copies[ch * (ny - 1) + j - 1].wait_recv()
            source = core * ny + lax.rem(yc + ny - j, ny)
            block = mixed.at[ch, pl.ds(pl.multiple_of(source * 64, 64), 64)]
            copy = remote(block, block, f_send.at[ch, j], f_recv.at[ch, j], sib)
            copy.start()
            f_copies.append(copy)

    load_i.wait()
    for ch in range(nch):
        for j in range(ny):
            f_copies[ch if j == 0 else nch + ch * (ny - 1) + j - 1].wait_recv()

        def finish(b, carry):
            rows = pl.ds(pl.multiple_of(b * 256, 256), 256)
            lanes = slice(ch * lc, (ch + 1) * lc)
            base = jnp.concatenate([conv[ch * tiles + t, rows, :] for t in range(tiles)], axis=1)
            value = dot(gmat[rows, :], mixed[ch]) + base
            value = 0.5 * value * (1.0 + lax.erf(value * (0.5**0.5)))
            out[pl.ds(b * 32, 32), :, lanes] = value.reshape(32, 8, lc).astype(BF16)
            return carry

        lax.fori_loop(0, 4, finish, 0)

    for copy in c_copies + r_copies + a_copies + f_copies:
        copy.wait_send()
    for (there, _, _, _), y_copy, k_copy in zip(pairs, y_copies, k_copies):

        @pl.when(there)
        def _(y_copy=y_copy, k_copy=k_copy):
            y_copy.wait_send()
            k_copy.wait_send()


def shards(field, conv_weight, conv_bias, spectral_weight):
    cells_x, cells_y, width = field.shape
    groups = lax.axis_size("gx")
    modes = spectral_weight.shape[0]
    ny = groups // 2
    lc = width // CHUNKS
    ftab, itab = expanded_tables(cells_x * groups, modes, groups, cells_y)
    dma = pltpu.SemaphoreType.DMA
    vmem = pltpu.VMEM
    scratch = [
        vmem((3, cells_x + 2, cells_y, width), BF16),
        vmem((64, 1024), BF16),
        vmem((27, 32, 32), BF16),
        vmem((4, 2, 32, 32), BF16),
        vmem((1, 32), F32),
        vmem((512, 1024), BF16),
        vmem((1024, 512), BF16),
        vmem((864, 256), F32),
        vmem((2304, 256), BF16),
        vmem((2304, 256), BF16),
        vmem((4, 256, 256), BF16),
        vmem((4, 1024, 128), F32),
        vmem((CHUNKS, 512, lc), F32),
        vmem((CHUNKS, 256, lc), BF16),
        vmem((CHUNKS, 256, lc), BF16),
        vmem((CHUNKS, 256, lc), BF16),
        vmem((CHUNKS, ny - 1, 64, lc), BF16),
        vmem((CHUNKS, 512, lc), BF16),
        vmem((2, 128, 512), BF16),
        vmem((2, 128, 512), BF16),
        vmem((2, 2, 8, 512), BF16),
        vmem((2, 2, 2, 8, 512), BF16),
        dma((6,)), dma((1,)),
        dma((CHUNKS,)), dma((CHUNKS,)),
        dma((CHUNKS, ny - 1)), dma((CHUNKS, ny - 1)),
        dma((CHUNKS, ny - 1)), dma((CHUNKS, ny - 1)),
        dma((CHUNKS, ny)), dma((CHUNKS, ny)),
        dma((2,)), dma((2,)), dma((2,)), dma((2,)), dma((2,)), dma((2,)),
        pltpu.SemaphoreType.REGULAR((2,)),
    ]
    operands = (field, conv_weight, conv_bias.reshape(1, -1), spectral_weight, ftab, itab)
    in_hbm = pl.BlockSpec(memory_space=pltpu.HBM)
    return pl.pallas_call(
        layer_kernel,
        out_shape=jax.ShapeDtypeStruct(field.shape, BF16),
        in_specs=[in_hbm] * 6,
        out_specs=pl.BlockSpec(memory_space=pltpu.VMEM),
        scratch_shapes=scratch,
        compiler_params=pltpu.CompilerParams(
            collective_id=0, has_side_effects=True, vmem_limit_bytes=40 * 1024 * 1024
        ),
        name="layer",
    )(*(pltpu.with_memory_space_constraint(a, pltpu.HBM) for a in operands))


def solution(mesh):
    placed = (P("gx", "gy", None), P(), P(), P())
    return jax.shard_map(
        shards, mesh=mesh, in_specs=placed, out_specs=P("gx", "gy", None), check_vma=False
    )
```

```python
import functools
import math

import jax
import jax.numpy as jnp
import numpy as np
from jax import lax
from jax.experimental import pallas as pl
from jax.experimental.pallas import tpu as pltpu
from jax.sharding import PartitionSpec as P

MESH = pl.DeviceIdType.MESH
CHUNKS = 2
SPLIT_ROW = 96
FIRST_BANDS = 0
SHARE = ((SPLIT_ROW, 128 - SPLIT_ROW), (0, SPLIT_ROW))
FAR_FIRST = (1, 0, 2)
F32 = jnp.float32
BF16 = jnp.bfloat16


def dot(a, b):
    return jnp.dot(a, b, preferred_element_type=F32)


def expanded_tables(length, modes, groups, rows_y):
    turns = (np.arange(modes)[:, None] * np.arange(length)[None, :]) % length
    angles = turns.astype(np.float32) * np.float32(2.0 * math.pi / length)
    pairs = np.stack([np.cos(angles), -np.sin(angles)], axis=1) * np.float32(1.0 / math.sqrt(length))
    doubling = np.where(np.arange(modes) == 0, 1.0, 2.0).astype(np.float32)
    forward = pairs.reshape(2 * modes, groups, length // groups).transpose(1, 0, 2)
    inverse = (pairs * doubling[:, None, None]).reshape(2 * modes, groups, length // groups).transpose(1, 2, 0)
    forward = np.repeat(forward, rows_y, axis=2)
    inverse = np.kron(inverse, np.eye(rows_y, dtype=np.float32))
    return jnp.asarray(forward, BF16), jnp.asarray(inverse, BF16)


def spread(table_ref, out_ref):
    rows, lanes = table_ref.shape

    def body(i, carry):
        part = table_ref[pl.ds(pl.multiple_of(i * 16, 16), 16), :].astype(F32)
        wide = jnp.broadcast_to(part[:, None, :], (16, 8, lanes))
        keep = lax.broadcasted_iota(jnp.int32, (16, 8, lanes), 1) == (
            lax.broadcasted_iota(jnp.int32, (16, 8, lanes), 2) & 7
        )
        out_ref[pl.ds(pl.multiple_of(i * 128, 128), 128), :] = (
            jnp.where(keep, wide, 0.0).reshape(128, lanes).astype(BF16)
        )
        return carry

    lax.fori_loop(0, rows // 16, body, 0)


def layer_kernel(
    field, convw, bias, specw, ftab, itab, out,
    fs, fexp, cw, sw, bv, amat, gmat, wrep, tmat, cmat, rmat, conv,
    part, cbuf, cland, rland, mixed, ybuf, yland, xland, cornl,
    load_sem, bar_send, c_send, c_recv, r_send, r_recv, a_send, a_recv, f_send, f_recv,
    x_send, x_recv, y_send, y_recv, k_send, k_recv, ready,
):
    nch, _, lc = mixed.shape
    tiles = lc // 128
    g = lax.axis_index("gx")
    h = lax.axis_index("gy")
    ng = lax.axis_size("gx")
    nh = lax.axis_size("gy")
    ny = ng // 2
    yc, core = g // 2, g % 2
    sib = (2 * yc + (1 - core), h)

    def ychip(j):
        return (2 * lax.rem(yc + j, ny) + core, h)

    left, right = lax.rem(g + ng - 1, ng), lax.rem(g + 1, ng)
    prev, nxt = lax.rem(h + nh - 1, nh), lax.rem(h + 1, nh)
    outer = lax.rem(g + ng + 2 * core - 1, ng)

    def remote(src, dst, s, r, dev):
        return pltpu.make_async_remote_copy(
            src_ref=src, dst_ref=dst, send_sem=s, recv_sem=r, device_id=dev, device_id_type=MESH
        )

    load_f = pltpu.make_async_copy(ftab.at[g], fexp, load_sem.at[0])
    load_x = pltpu.make_async_copy(field, fs.at[1, pl.ds(1, 128)], load_sem.at[1])
    load_i = pltpu.make_async_copy(itab.at[g], gmat, load_sem.at[2])
    load_w = pltpu.make_async_copy(convw, cw, load_sem.at[3])
    load_s = pltpu.make_async_copy(specw.at[pl.ds(8 * yc, 8)], sw, load_sem.at[4])
    load_b = pltpu.make_async_copy(bias, bv, load_sem.at[5])
    for load in (load_f, load_x, load_w, load_s, load_b, load_i):
        load.start()

    barrier = pltpu.get_barrier_semaphore()
    chips = [ychip(j) for j in range(1, ny)]
    for dev in [sib, (outer, h)] + chips:
        pl.semaphore_signal(barrier, inc=1, device_id=dev, device_id_type=MESH)
    first_up = lax.rem(h + 1, 8) != 0
    first_down = lax.rem(h, 8) == 0
    has_up, has_down = h < nh - 1, h > 0
    pairs = [
        (has_down, first_down, (g, prev), 1),
        (has_up, first_up, (g, nxt), 0),
    ]
    waits = jnp.int32(2 + len(chips))
    for there, first, dev, _ in pairs:

        @pl.when(there & first)
        def _(dev=dev):
            pl.semaphore_signal(barrier, inc=1, device_id=dev, device_id_type=MESH)

        waits = waits + jnp.where(there & ~first, 1, 0)

    load_f.wait()
    spread(fexp, amat)
    load_w.wait()
    rep8 = jnp.where(
        (lax.broadcasted_iota(jnp.int32, (32, 256), 1) & 31) == lax.broadcasted_iota(jnp.int32, (32, 256), 0), 1.0, 0.0
    ).astype(BF16)
    wrep[...] = dot(cw[...].reshape(864, 32), rep8)
    zlane8 = lax.broadcasted_iota(jnp.int32, (32, 256), 1) // 32
    cmat[...] = jnp.zeros_like(cmat)

    def band(t, carry):
        dyi, dxi = t // 3, t % 3
        base = pl.multiple_of((dxi * 3 + dyi) * 96, 32)
        w = [wrep[pl.ds(pl.multiple_of(base + 32 * k, 32), 32), :] for k in range(3)]
        for z in range(8):
            block = jnp.where(zlane8 == z + 1, w[0], 0.0)
            block = jnp.where(zlane8 == z, w[1], block)
            block = jnp.where(zlane8 == z - 1, w[2], block)
            tmat[pl.ds(pl.multiple_of(t * 256 + z * 32, 32), 32), :] = block.astype(BF16)
        cmat[pl.ds(pl.multiple_of(t * 256 + 96, 32), 32), :] = jnp.where(zlane8 == 4, w[0], 0.0).astype(BF16)
        cmat[pl.ds(pl.multiple_of(t * 256 + 128, 32), 32), :] = jnp.where(zlane8 == 3, w[2], 0.0).astype(BF16)
        return carry

    lax.fori_loop(0, FIRST_BANDS, band, 0)
    load_x.wait()
    def rows_of(chip, c):
        return pl.ds(pl.multiple_of(chip * 128 + SHARE[c][0], 16), SHARE[c][1])

    def aims(j, c):
        return rows_of(lax.rem(yc + j, ny), c)

    order = [(ch, j) for ch in range(nch) for j in (2, 1, 3)] + [(ch, 0) for ch in range(nch)]

    def c_copy(ch, j, owner):
        return remote(cbuf.at[ch, aims(j, owner)], cland.at[ch, aims(j, owner)], c_send.at[ch, j], c_recv.at[ch, j], sib)

    def r_copy(ch, j, c):
        return remote(
            cbuf.at[ch, aims(j, c)], rland.at[ch, j - 1, pl.ds(*SHARE[c])],
            r_send.at[ch, j - 1], r_recv.at[ch, j - 1], ychip(j),
        )

    def a_copy(ch, j, c):
        block = mixed.at[ch, aims(0, c)]
        return remote(block, block, a_send.at[ch, j - 1], a_recv.at[ch, j - 1], ychip(j))

    def f_copy(ch, j, c):
        block = mixed.at[ch, aims(ny - j, c)]
        return remote(block, block, f_send.at[ch, j], f_recv.at[ch, j], sib)

    value = dot(amat[...], fs[1, 1:129].reshape(1024, 512))
    for ch in range(nch):
        part[ch] = value[:, ch * lc : (ch + 1) * lc]
    pl.semaphore_wait(barrier, waits)

    def send_sums(c):
        for ch, j in order:
            cbuf[ch, aims(j, 1 - c), :] = part[ch, aims(j, 1 - c), :].astype(BF16)
            c_copy(ch, j, 1 - c).start()

    for c in range(2):
        pl.when(core == c)(functools.partial(send_sums, c))

    for there, first, dev, lands in pairs:

        @pl.when(there & ~first)
        def _(dev=dev, lands=lands):
            pl.semaphore_signal(ready.at[lands], inc=1, device_id=dev, device_id_type=MESH)

    x_copies = [
        remote(fs.at[1, pl.ds(127, 2)], xland.at[0], x_send.at[0], x_recv.at[0], (right, h)),
        remote(fs.at[1, pl.ds(1, 2)], xland.at[1], x_send.at[1], x_recv.at[1], (left, h)),
    ]
    for copy in x_copies:
        copy.start()
    def pass_sums(c):
        for ch, j in order:
            c_copy(ch, j, c).wait_recv()
            if j > 0:
                total = part[ch, aims(j, c), :] + cland[ch, aims(j, c), :].astype(F32)
                cbuf[ch, aims(j, c), :] = total.astype(BF16)
                r_copy(ch, j, c).start()

    for c in range(2):
        pl.when(core == c)(functools.partial(pass_sums, c))

    load_s.wait()

    def modes_of(c):
        return range(SHARE[c][0] // 16, (SHARE[c][0] + SHARE[c][1]) // 16)

    def mixing_weights(c):
        rep4 = jnp.where(
            (lax.broadcasted_iota(jnp.int32, (32, 128), 1) & 31) == lax.broadcasted_iota(jnp.int32, (32, 128), 0), 1.0, 0.0
        ).astype(BF16)
        sv = dot(sw[...].reshape(512, 32), rep4)
        zlane = lax.broadcasted_iota(jnp.int32, (32, 128), 1) // 32
        for m in modes_of(c):
            wr = sv[m * 64 : m * 64 + 32]
            wi = sv[m * 64 + 32 : m * 64 + 64]
            for r in range(2):
                for z in range(4):
                    first = jnp.where(zlane == z, wr if r == 0 else -wi, 0.0)
                    second = jnp.where(zlane == z, wi if r == 0 else wr, 0.0)
                    rmat[m, r * 128 + z * 32 : r * 128 + z * 32 + 32, :] = jnp.concatenate([first, second], axis=1).astype(BF16)

    for c in range(2):
        pl.when(core == c)(functools.partial(mixing_weights, c))

    row = lax.broadcasted_iota(jnp.int32, (64, 256), 0)
    col = lax.broadcasted_iota(jnp.int32, (64, 256), 1)
    pick = jnp.where(col == (row & 31) * 8 + jnp.where(row < 32, 7, 0), 1.0, 0.0).astype(BF16)
    for b in range(4):
        cells = fs[1, 1 + 32 * b : 33 + 32 * b].reshape(256, 512)
        picked = dot(pick, cells).astype(BF16)
        ybuf[0, 32 * b : 32 * b + 32, :] = picked[:32]
        ybuf[1, 32 * b : 32 * b + 32, :] = picked[32:]
    y_copies = [
        remote(ybuf.at[1], yland.at[1], y_send.at[1], y_recv.at[1], (g, prev)),
        remote(ybuf.at[0], yland.at[0], y_send.at[0], y_recv.at[0], (g, nxt)),
    ]
    k_copies = [
        remote(xland, cornl.at[1], k_send.at[1], k_recv.at[1], (g, prev)),
        remote(xland, cornl.at[0], k_send.at[0], k_recv.at[0], (g, nxt)),
    ]
    for (there, first, _, _), copy in zip(pairs, y_copies):
        pl.when(there & ~first)(copy.start)

    lax.fori_loop(FIRST_BANDS, 9, band, 0)

    def shift(first, count):
        cells = fs[1, pl.ds(first, count)].astype(F32)
        sub = lax.broadcasted_iota(jnp.int32, cells.shape, 1)
        fs[0, pl.ds(first, count)] = jnp.where(sub == 0, 0.0, pltpu.roll(cells, 1, 1)).astype(BF16)
        fs[2, pl.ds(first, count)] = jnp.where(sub == 7, 0.0, pltpu.roll(cells, 7, 1)).astype(BF16)

    def shift_block(b, carry):
        shift(1 + b * 32, 32)
        return carry

    lax.fori_loop(0, 4, shift_block, 0)
    for copy in x_copies:
        copy.wait()
    has_left = jnp.where(g > 0, 1.0, 0.0)
    has_right = jnp.where(g < ng - 1, 1.0, 0.0)
    for (there, first, _, _), copy in zip(pairs, k_copies):
        pl.when(there & ~first)(copy.start)

    def greet_later(far):
        k = 0 if far else 1
        there, first, _, _ = pairs[k]

        @pl.when(there & first)
        def _():
            pl.semaphore_wait(ready.at[k], 1)
            y_copies[k].start()
            k_copies[k].start()

    greet_later(False)
    fs[1, 0:1] = (xland[0, 1:2].astype(F32) * has_left).astype(BF16)
    fs[1, 129:130] = (xland[1, 0:1].astype(F32) * has_right).astype(BF16)
    shift(0, 1)
    shift(129, 1)

    load_b.wait()
    bias_row = jnp.concatenate([bv[...]] * 16, axis=1)

    def windows(taps, first, count):
        low = jnp.concatenate([t[:, :256] for t in taps], axis=1)
        high = jnp.concatenate([t[:, 256:] for t in taps], axis=1)
        mid = jnp.concatenate([t[:, 128:384] for t in taps], axis=1)
        rows = low.shape[0]
        main = dot(jnp.concatenate([low, high], axis=0), tmat[first : first + count, :])
        cross = dot(mid, cmat[first : first + count, :])
        return jnp.concatenate(
            [
                main[:rows, :128], main[:rows, 128:] + cross[:, :128],
                main[rows:, :128] + cross[:, 128:], main[rows:, 128:],
            ],
            axis=1,
        )

    def conv_block(b, carry):
        taps = [fs[dy, pl.ds(b * 32 + dx, 32)].reshape(256, 512) for dy in range(3) for dx in range(3)]
        value = windows(taps, 0, 2304) + bias_row
        for t in range(4):
            conv[t, pl.ds(pl.multiple_of(b * 256, 256), 256), :] = value[:, 128 * t : 128 * t + 128]
        return carry

    lax.fori_loop(0, 2, conv_block, 0, unroll=True)

    def mix_modes(c):
        first, count = SHARE[c]
        for ch in range(nch):
            coef = part[ch, aims(0, c), :] + cland[ch, aims(0, c), :].astype(F32)
            for j in range(1, ny):
                r_copy(ch, j, c).wait_recv()
                coef = coef + rland[ch, j - 1, first : first + count, :].astype(F32)
            pieces = []
            for m in modes_of(c):
                at = m * 16 - first
                rows = jnp.concatenate(
                    [
                        jnp.concatenate(
                            [coef[at + 8 * r : at + 8 * r + 8, 128 * t : 128 * t + 128] for r in range(2)], axis=1
                        )
                        for t in range(tiles)
                    ],
                    axis=0,
                ).astype(BF16)
                mix = dot(rows, rmat[m])
                for r in range(2):
                    pieces.append(
                        jnp.concatenate([mix[8 * t : 8 * t + 8, 128 * r : 128 * r + 128] for t in range(tiles)], axis=1)
                    )
            mixed[ch, aims(0, c), :] = jnp.concatenate(pieces, axis=0).astype(BF16)
            for k in FAR_FIRST:
                a_copy(ch, k + 1, c).start()
            f_copy(ch, 0, c).start()

    for c in range(2):
        pl.when(core == c)(functools.partial(mix_modes, c))

    greet_later(True)

    lax.fori_loop(2, 4, conv_block, 0, unroll=True)

    row = lax.broadcasted_iota(jnp.int32, (256, 160), 0)
    col = lax.broadcasted_iota(jnp.int32, (256, 160), 1)
    x = row & 127
    def halo(side, here):
        @pl.when(pairs[side][0] & here)
        def _():
            y_copies[1 - side].wait_recv()
            k_copies[1 - side].wait_recv()
            yrow = 7 if side == 0 else 0
            inside = jnp.where(row < 128, x - 1, x + 1)
            picks = jnp.where((col == inside) & (col < 128), 1.0, 0.0)
            picks = jnp.where((row == 0) & (col == 128 + 8 + yrow), has_left, picks)
            picks = jnp.where((row == 255) & (col == 128 + 16 + yrow), has_right, picks)
            mid_rows = yland[side]
            source = jnp.concatenate([mid_rows, cornl[side].reshape(32, 512)], axis=0)
            moved = dot(picks.astype(BF16), source).astype(BF16)
            value = windows([moved[:128], mid_rows, moved[128:]], 1536 * side, 768)
            edge = pl.ds(0 if side == 0 else 7, 128, stride=8)
            for t in range(4):
                conv[t, edge, :] = conv[t, edge, :] + value[:, 128 * t : 128 * t + 128]

    far_first = lax.rem(h, 8) == 0
    halo(1, h >= 0)
    halo(0, ~far_first)

    def pass_mixed(c):
        for ch in range(nch):
            for j in (1, 3, 2):
                a_copy(ch, j, c).wait_recv()
                f_copy(ch, j, c).start()

    for c in range(2):
        pl.when(core == c)(functools.partial(pass_mixed, c))

    halo(0, far_first)

    load_i.wait()
    for ch in range(nch):

        def wait_mixed(c, ch=ch):
            for j in range(ny):
                f_copy(ch, j, 1 - c).wait_recv()

        for c in range(2):
            pl.when(core == c)(functools.partial(wait_mixed, c))

        def finish(b, carry):
            rows = pl.ds(pl.multiple_of(b * 256, 256), 256)
            lanes = slice(ch * lc, (ch + 1) * lc)
            base = jnp.concatenate([conv[ch * tiles + t, rows, :] for t in range(tiles)], axis=1)
            value = dot(gmat[rows, :], mixed[ch]) + base
            value = 0.5 * value * (1.0 + lax.erf(value * (0.5**0.5)))
            out[pl.ds(b * 32, 32), :, lanes] = value.reshape(32, 8, lc).astype(BF16)
            return carry

        lax.fori_loop(0, 4, finish, 0, unroll=True)

    def wait_sends(c):
        for ch in range(nch):
            for j in range(ny):
                c_copy(ch, j, 1 - c).wait_send()
                f_copy(ch, j, c).wait_send()
            for j in range(1, ny):
                r_copy(ch, j, c).wait_send()
                a_copy(ch, j, c).wait_send()

    for c in range(2):
        pl.when(core == c)(functools.partial(wait_sends, c))

    for (there, _, _, _), y_copy, k_copy in zip(pairs, y_copies, k_copies):

        @pl.when(there)
        def _(y_copy=y_copy, k_copy=k_copy):
            y_copy.wait_send()
            k_copy.wait_send()


def shards(field, conv_weight, conv_bias, spectral_weight):
    cells_x, cells_y, width = field.shape
    groups = lax.axis_size("gx")
    modes = spectral_weight.shape[0]
    ny = groups // 2
    lc = width // CHUNKS
    ftab, itab = expanded_tables(cells_x * groups, modes, groups, cells_y)
    dma = pltpu.SemaphoreType.DMA
    vmem = pltpu.VMEM
    scratch = [
        vmem((3, cells_x + 2, cells_y, width), BF16),
        vmem((64, 1024), BF16),
        vmem((27, 32, 32), BF16),
        vmem((8, 2, 32, 32), BF16),
        vmem((1, 32), F32),
        vmem((512, 1024), BF16),
        vmem((1024, 512), BF16),
        vmem((864, 256), F32),
        vmem((2304, 256), BF16),
        vmem((2304, 256), BF16),
        vmem((8, 256, 256), BF16),
        vmem((4, 1024, 128), F32),
        vmem((CHUNKS, 512, lc), F32),
        vmem((CHUNKS, 512, lc), BF16),
        vmem((CHUNKS, 512, lc), BF16),
        vmem((CHUNKS, ny - 1, 128, lc), BF16),
        vmem((CHUNKS, 512, lc), BF16),
        vmem((2, 128, 512), BF16),
        vmem((2, 128, 512), BF16),
        vmem((2, 2, 8, 512), BF16),
        vmem((2, 2, 2, 8, 512), BF16),
        dma((6,)), dma((1,)),
        dma((CHUNKS, ny)), dma((CHUNKS, ny)),
        dma((CHUNKS, ny - 1)), dma((CHUNKS, ny - 1)),
        dma((CHUNKS, ny - 1)), dma((CHUNKS, ny - 1)),
        dma((CHUNKS, ny)), dma((CHUNKS, ny)),
        dma((2,)), dma((2,)), dma((2,)), dma((2,)), dma((2,)), dma((2,)),
        pltpu.SemaphoreType.REGULAR((2,)),
    ]
    operands = (field, conv_weight, conv_bias.reshape(1, -1), spectral_weight, ftab, itab)
    in_hbm = pl.BlockSpec(memory_space=pltpu.HBM)
    return pl.pallas_call(
        layer_kernel,
        out_shape=jax.ShapeDtypeStruct(field.shape, BF16),
        in_specs=[in_hbm] * 6,
        out_specs=pl.BlockSpec(memory_space=pltpu.VMEM),
        scratch_shapes=scratch,
        compiler_params=pltpu.CompilerParams(
            collective_id=0, has_side_effects=True, vmem_limit_bytes=40 * 1024 * 1024
        ),
        name="layer",
    )(*(pltpu.with_memory_space_constraint(a, pltpu.HBM) for a in operands))


def solution(mesh):
    placed = (P("gx", "gy", None), P(), P(), P())
    return jax.shard_map(
        shards, mesh=mesh, in_specs=placed, out_specs=P("gx", "gy", None), check_vma=False
    )
```

```python
import functools
import math

import jax
import jax.numpy as jnp
import numpy as np
from jax import lax
from jax.experimental import pallas as pl
from jax.experimental.pallas import tpu as pltpu
from jax.sharding import PartitionSpec as P

MESH = pl.DeviceIdType.MESH
CHUNKS = 2
SPLIT_ROW = 96
FIRST_BANDS = 0
SHARE = ((SPLIT_ROW, 128 - SPLIT_ROW), (0, SPLIT_ROW))
FAR_FIRST = (1, 0, 2)
F32 = jnp.float32
BF16 = jnp.bfloat16


def dot(a, b):
    return jnp.dot(a, b, preferred_element_type=F32)


def expanded_tables(length, modes, groups, rows_y):
    turns = (np.arange(modes)[:, None] * np.arange(length)[None, :]) % length
    angles = turns.astype(np.float32) * np.float32(2.0 * math.pi / length)
    pairs = np.stack([np.cos(angles), -np.sin(angles)], axis=1) * np.float32(1.0 / math.sqrt(length))
    doubling = np.where(np.arange(modes) == 0, 1.0, 2.0).astype(np.float32)
    forward = pairs.reshape(2 * modes, groups, length // groups).transpose(1, 0, 2)
    inverse = (pairs * doubling[:, None, None]).reshape(2 * modes, groups, length // groups).transpose(1, 2, 0)
    forward = np.repeat(forward, rows_y, axis=2)
    inverse = np.kron(inverse, np.eye(rows_y, dtype=np.float32))
    return jnp.asarray(forward, BF16), jnp.asarray(inverse, BF16)


def spread(table_ref, out_ref):
    rows, lanes = table_ref.shape

    def body(i, carry):
        part = table_ref[pl.ds(pl.multiple_of(i * 16, 16), 16), :].astype(F32)
        wide = jnp.broadcast_to(part[:, None, :], (16, 8, lanes))
        keep = lax.broadcasted_iota(jnp.int32, (16, 8, lanes), 1) == (
            lax.broadcasted_iota(jnp.int32, (16, 8, lanes), 2) & 7
        )
        out_ref[pl.ds(pl.multiple_of(i * 128, 128), 128), :] = (
            jnp.where(keep, wide, 0.0).reshape(128, lanes).astype(BF16)
        )
        return carry

    lax.fori_loop(0, rows // 16, body, 0)


def layer_kernel(
    field, convw, bias, specw, ftab, itab, out,
    fs, fexp, cw, sw, bv, amat, gmat, wrep, tmat, cmat, rmat, conv,
    part, cbuf, cland, rland, mixed, ybuf, yland, xland, cornl,
    load_sem, bar_send, c_send, c_recv, r_send, r_recv, a_send, a_recv, f_send, f_recv,
    x_send, x_recv, y_send, y_recv, k_send, k_recv, ready,
):
    nch, _, lc = mixed.shape
    tiles = lc // 128
    g = lax.axis_index("gx")
    h = lax.axis_index("gy")
    ng = lax.axis_size("gx")
    nh = lax.axis_size("gy")
    ny = ng // 2
    yc, core = g // 2, g % 2
    sib = (2 * yc + (1 - core), h)

    def ychip(j):
        return (2 * lax.rem(yc + j, ny) + core, h)

    left, right = lax.rem(g + ng - 1, ng), lax.rem(g + 1, ng)
    prev, nxt = lax.rem(h + nh - 1, nh), lax.rem(h + 1, nh)
    outer = lax.rem(g + ng + 2 * core - 1, ng)

    def remote(src, dst, s, r, dev):
        return pltpu.make_async_remote_copy(
            src_ref=src, dst_ref=dst, send_sem=s, recv_sem=r, device_id=dev, device_id_type=MESH
        )

    load_f = pltpu.make_async_copy(ftab.at[g], fexp, load_sem.at[0])
    load_x = pltpu.make_async_copy(field, fs.at[1, pl.ds(1, 128)], load_sem.at[1])
    load_i = pltpu.make_async_copy(itab.at[g], gmat, load_sem.at[2])
    load_w = pltpu.make_async_copy(convw, cw, load_sem.at[3])
    load_s = pltpu.make_async_copy(specw.at[pl.ds(8 * yc, 8)], sw, load_sem.at[4])
    load_b = pltpu.make_async_copy(bias, bv, load_sem.at[5])
    for load in (load_f, load_x, load_w, load_s, load_b, load_i):
        load.start()

    barrier = pltpu.get_barrier_semaphore()
    chips = [ychip(j) for j in range(1, ny)]
    for dev in [sib, (outer, h)] + chips:
        pl.semaphore_signal(barrier, inc=1, device_id=dev, device_id_type=MESH)
    first_up = lax.rem(h + 1, 8) != 0
    first_down = lax.rem(h, 8) == 0
    has_up, has_down = h < nh - 1, h > 0
    pairs = [
        (has_down, first_down, (g, prev), 1),
        (has_up, first_up, (g, nxt), 0),
    ]
    waits = jnp.int32(2 + len(chips))
    for there, first, dev, _ in pairs:

        @pl.when(there & first)
        def _(dev=dev):
            pl.semaphore_signal(barrier, inc=1, device_id=dev, device_id_type=MESH)

        waits = waits + jnp.where(there & ~first, 1, 0)

    load_f.wait()
    spread(fexp, amat)
    load_w.wait()
    rep8 = jnp.where(
        (lax.broadcasted_iota(jnp.int32, (32, 256), 1) & 31) == lax.broadcasted_iota(jnp.int32, (32, 256), 0), 1.0, 0.0
    ).astype(BF16)
    wrep[...] = dot(cw[...].reshape(864, 32), rep8)
    zlane8 = lax.broadcasted_iota(jnp.int32, (32, 256), 1) // 32
    cmat[...] = jnp.zeros_like(cmat)

    def band(t, carry):
        dyi, dxi = t // 3, t % 3
        base = pl.multiple_of((dxi * 3 + dyi) * 96, 32)
        w = [wrep[pl.ds(pl.multiple_of(base + 32 * k, 32), 32), :] for k in range(3)]
        for z in range(8):
            block = jnp.where(zlane8 == z + 1, w[0], 0.0)
            block = jnp.where(zlane8 == z, w[1], block)
            block = jnp.where(zlane8 == z - 1, w[2], block)
            tmat[pl.ds(pl.multiple_of(t * 256 + z * 32, 32), 32), :] = block.astype(BF16)
        cmat[pl.ds(pl.multiple_of(t * 256 + 96, 32), 32), :] = jnp.where(zlane8 == 4, w[0], 0.0).astype(BF16)
        cmat[pl.ds(pl.multiple_of(t * 256 + 128, 32), 32), :] = jnp.where(zlane8 == 3, w[2], 0.0).astype(BF16)
        return carry

    lax.fori_loop(0, FIRST_BANDS, band, 0)
    load_x.wait()
    def rows_of(chip, c):
        return pl.ds(pl.multiple_of(chip * 128 + SHARE[c][0], 16), SHARE[c][1])

    def aims(j, c):
        return rows_of(lax.rem(yc + j, ny), c)

    order = [(ch, j) for ch in range(nch) for j in (2, 1, 3)] + [(ch, 0) for ch in range(nch)]

    def c_copy(ch, j, owner):
        return remote(cbuf.at[ch, aims(j, owner)], cland.at[ch, aims(j, owner)], c_send.at[ch, j], c_recv.at[ch, j], sib)

    def r_copy(ch, j, c):
        return remote(
            cbuf.at[ch, aims(j, c)], rland.at[ch, j - 1, pl.ds(*SHARE[c])],
            r_send.at[ch, j - 1], r_recv.at[ch, j - 1], ychip(j),
        )

    def a_copy(ch, j, c):
        block = mixed.at[ch, aims(0, c)]
        return remote(block, block, a_send.at[ch, j - 1], a_recv.at[ch, j - 1], ychip(j))

    def f_copy(ch, j, c):
        block = mixed.at[ch, aims(ny - j, c)]
        return remote(block, block, f_send.at[ch, j], f_recv.at[ch, j], sib)

    value = dot(amat[...], fs[1, 1:129].reshape(1024, 512))
    for ch in range(nch):
        part[ch] = value[:, ch * lc : (ch + 1) * lc]
    pl.semaphore_wait(barrier, waits)

    def send_sums(c):
        for ch, j in order:
            cbuf[ch, aims(j, 1 - c), :] = part[ch, aims(j, 1 - c), :].astype(BF16)
            c_copy(ch, j, 1 - c).start()

    for c in range(2):
        pl.when(core == c)(functools.partial(send_sums, c))

    for there, first, dev, lands in pairs:

        @pl.when(there & ~first)
        def _(dev=dev, lands=lands):
            pl.semaphore_signal(ready.at[lands], inc=1, device_id=dev, device_id_type=MESH)

    x_copies = [
        remote(fs.at[1, pl.ds(127, 2)], xland.at[0], x_send.at[0], x_recv.at[0], (right, h)),
        remote(fs.at[1, pl.ds(1, 2)], xland.at[1], x_send.at[1], x_recv.at[1], (left, h)),
    ]
    for copy in x_copies:
        copy.start()
    def pass_sums(c):
        for ch, j in order:
            c_copy(ch, j, c).wait_recv()
            if j > 0:
                total = part[ch, aims(j, c), :] + cland[ch, aims(j, c), :].astype(F32)
                cbuf[ch, aims(j, c), :] = total.astype(BF16)
                r_copy(ch, j, c).start()

    for c in range(2):
        pl.when(core == c)(functools.partial(pass_sums, c))

    load_s.wait()

    def modes_of(c):
        return range(SHARE[c][0] // 16, (SHARE[c][0] + SHARE[c][1]) // 16)

    def mixing_weights(c):
        rep4 = jnp.where(
            (lax.broadcasted_iota(jnp.int32, (32, 128), 1) & 31) == lax.broadcasted_iota(jnp.int32, (32, 128), 0), 1.0, 0.0
        ).astype(BF16)
        sv = dot(sw[...].reshape(512, 32), rep4)
        zlane = lax.broadcasted_iota(jnp.int32, (32, 128), 1) // 32
        for m in modes_of(c):
            wr = sv[m * 64 : m * 64 + 32]
            wi = sv[m * 64 + 32 : m * 64 + 64]
            for r in range(2):
                for z in range(4):
                    first = jnp.where(zlane == z, wr if r == 0 else -wi, 0.0)
                    second = jnp.where(zlane == z, wi if r == 0 else wr, 0.0)
                    rmat[m, r * 128 + z * 32 : r * 128 + z * 32 + 32, :] = jnp.concatenate([first, second], axis=1).astype(BF16)

    for c in range(2):
        pl.when(core == c)(functools.partial(mixing_weights, c))

    row = lax.broadcasted_iota(jnp.int32, (64, 256), 0)
    col = lax.broadcasted_iota(jnp.int32, (64, 256), 1)
    pick = jnp.where(col == (row & 31) * 8 + jnp.where(row < 32, 7, 0), 1.0, 0.0).astype(BF16)
    for b in range(4):
        cells = fs[1, 1 + 32 * b : 33 + 32 * b].reshape(256, 512)
        picked = dot(pick, cells).astype(BF16)
        ybuf[0, 32 * b : 32 * b + 32, :] = picked[:32]
        ybuf[1, 32 * b : 32 * b + 32, :] = picked[32:]
    y_copies = [
        remote(ybuf.at[1], yland.at[1], y_send.at[1], y_recv.at[1], (g, prev)),
        remote(ybuf.at[0], yland.at[0], y_send.at[0], y_recv.at[0], (g, nxt)),
    ]
    k_copies = [
        remote(xland, cornl.at[1], k_send.at[1], k_recv.at[1], (g, prev)),
        remote(xland, cornl.at[0], k_send.at[0], k_recv.at[0], (g, nxt)),
    ]
    for (there, first, _, _), copy in zip(pairs, y_copies):
        pl.when(there & ~first)(copy.start)

    lax.fori_loop(FIRST_BANDS, 9, band, 0)

    def shift(first, count):
        cells = fs[1, pl.ds(first, count)].astype(F32)
        sub = lax.broadcasted_iota(jnp.int32, cells.shape, 1)
        fs[0, pl.ds(first, count)] = jnp.where(sub == 0, 0.0, pltpu.roll(cells, 1, 1)).astype(BF16)
        fs[2, pl.ds(first, count)] = jnp.where(sub == 7, 0.0, pltpu.roll(cells, 7, 1)).astype(BF16)

    def shift_block(b, carry):
        shift(1 + b * 32, 32)
        return carry

    lax.fori_loop(0, 4, shift_block, 0)
    for copy in x_copies:
        copy.wait()
    has_left = jnp.where(g > 0, 1.0, 0.0)
    has_right = jnp.where(g < ng - 1, 1.0, 0.0)
    for (there, first, _, _), copy in zip(pairs, k_copies):
        pl.when(there & ~first)(copy.start)

    def greet_later(far):
        k = 0 if far else 1
        there, first, _, _ = pairs[k]

        @pl.when(there & first)
        def _():
            pl.semaphore_wait(ready.at[k], 1)
            y_copies[k].start()
            k_copies[k].start()

    greet_later(False)
    fs[1, 0:1] = (xland[0, 1:2].astype(F32) * has_left).astype(BF16)
    fs[1, 129:130] = (xland[1, 0:1].astype(F32) * has_right).astype(BF16)
    shift(0, 1)
    shift(129, 1)

    load_b.wait()
    bias_row = jnp.concatenate([bv[...]] * 16, axis=1)

    def windows(taps, first, count):
        low = jnp.concatenate([t[:, :256] for t in taps], axis=1)
        high = jnp.concatenate([t[:, 256:] for t in taps], axis=1)
        mid = jnp.concatenate([t[:, 128:384] for t in taps], axis=1)
        rows = low.shape[0]
        main = dot(jnp.concatenate([low, high], axis=0), tmat[first : first + count, :])
        cross = dot(mid, cmat[first : first + count, :])
        return jnp.concatenate(
            [
                main[:rows, :128], main[:rows, 128:] + cross[:, :128],
                main[rows:, :128] + cross[:, 128:], main[rows:, 128:],
            ],
            axis=1,
        )

    def conv_block(b, carry):
        taps = [fs[dy, pl.ds(b * 32 + dx, 32)].reshape(256, 512) for dy in range(3) for dx in range(3)]
        value = windows(taps, 0, 2304) + bias_row
        for t in range(4):
            conv[t, pl.ds(pl.multiple_of(b * 256, 256), 256), :] = value[:, 128 * t : 128 * t + 128]
        return carry

    lax.fori_loop(0, 2, conv_block, 0, unroll=True)

    def mix_modes(c):
        first, count = SHARE[c]
        for ch in range(nch):
            coef = part[ch, aims(0, c), :] + cland[ch, aims(0, c), :].astype(F32)
            for j in range(1, ny):
                r_copy(ch, j, c).wait_recv()
                coef = coef + rland[ch, j - 1, first : first + count, :].astype(F32)
            pieces = []
            for m in modes_of(c):
                at = m * 16 - first
                rows = jnp.concatenate(
                    [
                        jnp.concatenate(
                            [coef[at + 8 * r : at + 8 * r + 8, 128 * t : 128 * t + 128] for r in range(2)], axis=1
                        )
                        for t in range(tiles)
                    ],
                    axis=0,
                ).astype(BF16)
                mix = dot(rows, rmat[m])
                for r in range(2):
                    pieces.append(
                        jnp.concatenate([mix[8 * t : 8 * t + 8, 128 * r : 128 * r + 128] for t in range(tiles)], axis=1)
                    )
            mixed[ch, aims(0, c), :] = jnp.concatenate(pieces, axis=0).astype(BF16)
            for k in FAR_FIRST:
                a_copy(ch, k + 1, c).start()
            f_copy(ch, 0, c).start()

    for c in range(2):
        pl.when(core == c)(functools.partial(mix_modes, c))

    lax.fori_loop(2, 4, conv_block, 0, unroll=True)
    greet_later(True)

    row = lax.broadcasted_iota(jnp.int32, (256, 160), 0)
    col = lax.broadcasted_iota(jnp.int32, (256, 160), 1)
    x = row & 127
    def halo(side, here):
        @pl.when(pairs[side][0] & here)
        def _():
            y_copies[1 - side].wait_recv()
            k_copies[1 - side].wait_recv()
            yrow = 7 if side == 0 else 0
            inside = jnp.where(row < 128, x - 1, x + 1)
            picks = jnp.where((col == inside) & (col < 128), 1.0, 0.0)
            picks = jnp.where((row == 0) & (col == 128 + 8 + yrow), has_left, picks)
            picks = jnp.where((row == 255) & (col == 128 + 16 + yrow), has_right, picks)
            mid_rows = yland[side]
            source = jnp.concatenate([mid_rows, cornl[side].reshape(32, 512)], axis=0)
            moved = dot(picks.astype(BF16), source).astype(BF16)
            value = windows([moved[:128], mid_rows, moved[128:]], 1536 * side, 768)
            edge = pl.ds(0 if side == 0 else 7, 128, stride=8)
            for t in range(4):
                conv[t, edge, :] = conv[t, edge, :] + value[:, 128 * t : 128 * t + 128]

    far_first = lax.rem(h, 8) == 0
    halo(1, h >= 0)
    halo(0, ~far_first)

    def pass_mixed(c):
        for ch in range(nch):
            for j in (1, 3, 2):
                a_copy(ch, j, c).wait_recv()
                f_copy(ch, j, c).start()

    for c in range(2):
        pl.when(core == c)(functools.partial(pass_mixed, c))

    halo(0, far_first)

    load_i.wait()
    for ch in range(nch):

        def wait_mixed(c, ch=ch):
            for j in range(ny):
                f_copy(ch, j, 1 - c).wait_recv()

        for c in range(2):
            pl.when(core == c)(functools.partial(wait_mixed, c))

        def finish(b, carry):
            rows = pl.ds(pl.multiple_of(b * 256, 256), 256)
            lanes = slice(ch * lc, (ch + 1) * lc)
            base = jnp.concatenate([conv[ch * tiles + t, rows, :] for t in range(tiles)], axis=1)
            value = dot(gmat[rows, :], mixed[ch]) + base
            value = 0.5 * value * (1.0 + lax.erf(value * (0.5**0.5)))
            out[pl.ds(b * 32, 32), :, lanes] = value.reshape(32, 8, lc).astype(BF16)
            return carry

        lax.fori_loop(0, 4, finish, 0, unroll=True)

    def wait_sends(c):
        for ch in range(nch):
            for j in range(ny):
                c_copy(ch, j, 1 - c).wait_send()
                f_copy(ch, j, c).wait_send()
            for j in range(1, ny):
                r_copy(ch, j, c).wait_send()
                a_copy(ch, j, c).wait_send()

    for c in range(2):
        pl.when(core == c)(functools.partial(wait_sends, c))

    for (there, _, _, _), y_copy, k_copy in zip(pairs, y_copies, k_copies):

        @pl.when(there)
        def _(y_copy=y_copy, k_copy=k_copy):
            y_copy.wait_send()
            k_copy.wait_send()


def shards(field, conv_weight, conv_bias, spectral_weight):
    cells_x, cells_y, width = field.shape
    groups = lax.axis_size("gx")
    modes = spectral_weight.shape[0]
    ny = groups // 2
    lc = width // CHUNKS
    ftab, itab = expanded_tables(cells_x * groups, modes, groups, cells_y)
    dma = pltpu.SemaphoreType.DMA
    vmem = pltpu.VMEM
    scratch = [
        vmem((3, cells_x + 2, cells_y, width), BF16),
        vmem((64, 1024), BF16),
        vmem((27, 32, 32), BF16),
        vmem((8, 2, 32, 32), BF16),
        vmem((1, 32), F32),
        vmem((512, 1024), BF16),
        vmem((1024, 512), BF16),
        vmem((864, 256), F32),
        vmem((2304, 256), BF16),
        vmem((2304, 256), BF16),
        vmem((8, 256, 256), BF16),
        vmem((4, 1024, 128), F32),
        vmem((CHUNKS, 512, lc), F32),
        vmem((CHUNKS, 512, lc), BF16),
        vmem((CHUNKS, 512, lc), BF16),
        vmem((CHUNKS, ny - 1, 128, lc), BF16),
        vmem((CHUNKS, 512, lc), BF16),
        vmem((2, 128, 512), BF16),
        vmem((2, 128, 512), BF16),
        vmem((2, 2, 8, 512), BF16),
        vmem((2, 2, 2, 8, 512), BF16),
        dma((6,)), dma((1,)),
        dma((CHUNKS, ny)), dma((CHUNKS, ny)),
        dma((CHUNKS, ny - 1)), dma((CHUNKS, ny - 1)),
        dma((CHUNKS, ny - 1)), dma((CHUNKS, ny - 1)),
        dma((CHUNKS, ny)), dma((CHUNKS, ny)),
        dma((2,)), dma((2,)), dma((2,)), dma((2,)), dma((2,)), dma((2,)),
        pltpu.SemaphoreType.REGULAR((2,)),
    ]
    operands = (field, conv_weight, conv_bias.reshape(1, -1), spectral_weight, ftab, itab)
    in_hbm = pl.BlockSpec(memory_space=pltpu.HBM)
    return pl.pallas_call(
        layer_kernel,
        out_shape=jax.ShapeDtypeStruct(field.shape, BF16),
        in_specs=[in_hbm] * 6,
        out_specs=pl.BlockSpec(memory_space=pltpu.VMEM),
        scratch_shapes=scratch,
        compiler_params=pltpu.CompilerParams(
            collective_id=0, has_side_effects=True, vmem_limit_bytes=40 * 1024 * 1024
        ),
        name="layer",
    )(*(pltpu.with_memory_space_constraint(a, pltpu.HBM) for a in operands))


def solution(mesh):
    placed = (P("gx", "gy", None), P(), P(), P())
    return jax.shard_map(
        shards, mesh=mesh, in_specs=placed, out_specs=P("gx", "gy", None), check_vma=False
    )
```

```python
import functools
import math

import jax
import jax.numpy as jnp
import numpy as np
from jax import lax
from jax.experimental import pallas as pl
from jax.experimental.pallas import tpu as pltpu
from jax.sharding import PartitionSpec as P

MESH = pl.DeviceIdType.MESH
CHUNKS = 2
SPLIT_ROW = 96
FIRST_BANDS = 0
SHARE = ((SPLIT_ROW, 128 - SPLIT_ROW), (0, SPLIT_ROW))
FAR_FIRST = (1, 0, 2)
F32 = jnp.float32
BF16 = jnp.bfloat16


def dot(a, b):
    return jnp.dot(a, b, preferred_element_type=F32)


def expanded_tables(length, modes, groups, rows_y):
    turns = (np.arange(modes)[:, None] * np.arange(length)[None, :]) % length
    angles = turns.astype(np.float32) * np.float32(2.0 * math.pi / length)
    pairs = np.stack([np.cos(angles), -np.sin(angles)], axis=1) * np.float32(1.0 / math.sqrt(length))
    doubling = np.where(np.arange(modes) == 0, 1.0, 2.0).astype(np.float32)
    forward = pairs.reshape(2 * modes, groups, length // groups).transpose(1, 0, 2)
    inverse = (pairs * doubling[:, None, None]).reshape(2 * modes, groups, length // groups).transpose(1, 2, 0)
    forward = np.repeat(forward, rows_y, axis=2)
    inverse = np.kron(inverse, np.eye(rows_y, dtype=np.float32))
    return jnp.asarray(forward, BF16), jnp.asarray(inverse, BF16)


def spread(table_ref, out_ref):
    rows, lanes = table_ref.shape

    def body(i, carry):
        part = table_ref[pl.ds(pl.multiple_of(i * 16, 16), 16), :].astype(F32)
        wide = jnp.broadcast_to(part[:, None, :], (16, 8, lanes))
        keep = lax.broadcasted_iota(jnp.int32, (16, 8, lanes), 1) == (
            lax.broadcasted_iota(jnp.int32, (16, 8, lanes), 2) & 7
        )
        out_ref[pl.ds(pl.multiple_of(i * 128, 128), 128), :] = (
            jnp.where(keep, wide, 0.0).reshape(128, lanes).astype(BF16)
        )
        return carry

    lax.fori_loop(0, rows // 16, body, 0)


def layer_kernel(
    field, convw, bias, specw, ftab, itab, out,
    fs, fexp, cw, sw, bv, amat, gmat, wrep, tmat, cmat, rmat, conv,
    part, cbuf, cland, rland, mixed, ybuf, yland, xland, cornl,
    load_sem, bar_send, c_send, c_recv, r_send, r_recv, a_send, a_recv, f_send, f_recv,
    x_send, x_recv, y_send, y_recv, k_send, k_recv, ready,
):
    nch, _, lc = mixed.shape
    tiles = lc // 128
    g = lax.axis_index("gx")
    h = lax.axis_index("gy")
    ng = lax.axis_size("gx")
    nh = lax.axis_size("gy")
    ny = ng // 2
    yc, core = g // 2, g % 2
    sib = (2 * yc + (1 - core), h)

    def ychip(j):
        return (2 * lax.rem(yc + j, ny) + core, h)

    left, right = lax.rem(g + ng - 1, ng), lax.rem(g + 1, ng)
    prev, nxt = lax.rem(h + nh - 1, nh), lax.rem(h + 1, nh)
    outer = lax.rem(g + ng + 2 * core - 1, ng)

    def remote(src, dst, s, r, dev):
        return pltpu.make_async_remote_copy(
            src_ref=src, dst_ref=dst, send_sem=s, recv_sem=r, device_id=dev, device_id_type=MESH
        )

    load_f = pltpu.make_async_copy(ftab.at[g], fexp, load_sem.at[0])
    load_x = pltpu.make_async_copy(field, fs.at[1, pl.ds(1, 128)], load_sem.at[1])
    load_i = pltpu.make_async_copy(itab.at[g], gmat, load_sem.at[2])
    load_w = pltpu.make_async_copy(convw, cw, load_sem.at[3])
    load_s = pltpu.make_async_copy(specw.at[pl.ds(8 * yc, 8)], sw, load_sem.at[4])
    load_b = pltpu.make_async_copy(bias, bv, load_sem.at[5])
    for load in (load_f, load_x, load_w, load_s, load_b, load_i):
        load.start()

    barrier = pltpu.get_barrier_semaphore()
    chips = [ychip(j) for j in range(1, ny)]
    for dev in [sib, (outer, h)] + chips:
        pl.semaphore_signal(barrier, inc=1, device_id=dev, device_id_type=MESH)
    first_up = lax.rem(h + 1, 8) != 0
    first_down = lax.rem(h, 8) == 0
    has_up, has_down = h < nh - 1, h > 0
    pairs = [
        (has_down, first_down, (g, prev), 1),
        (has_up, first_up, (g, nxt), 0),
    ]
    waits = jnp.int32(2 + len(chips))
    for there, first, dev, _ in pairs:

        @pl.when(there & first)
        def _(dev=dev):
            pl.semaphore_signal(barrier, inc=1, device_id=dev, device_id_type=MESH)

        waits = waits + jnp.where(there & ~first, 1, 0)

    load_f.wait()
    spread(fexp, amat)
    load_w.wait()
    rep8 = jnp.where(
        (lax.broadcasted_iota(jnp.int32, (32, 256), 1) & 31) == lax.broadcasted_iota(jnp.int32, (32, 256), 0), 1.0, 0.0
    ).astype(BF16)
    wrep[...] = dot(cw[...].reshape(864, 32), rep8)
    zlane8 = lax.broadcasted_iota(jnp.int32, (32, 256), 1) // 32
    cmat[...] = jnp.zeros_like(cmat)

    def band(t, carry):
        dyi, dxi = t // 3, t % 3
        base = pl.multiple_of((dxi * 3 + dyi) * 96, 32)
        w = [wrep[pl.ds(pl.multiple_of(base + 32 * k, 32), 32), :] for k in range(3)]
        for z in range(8):
            block = jnp.where(zlane8 == z + 1, w[0], 0.0)
            block = jnp.where(zlane8 == z, w[1], block)
            block = jnp.where(zlane8 == z - 1, w[2], block)
            tmat[pl.ds(pl.multiple_of(t * 256 + z * 32, 32), 32), :] = block.astype(BF16)
        cmat[pl.ds(pl.multiple_of(t * 256 + 96, 32), 32), :] = jnp.where(zlane8 == 4, w[0], 0.0).astype(BF16)
        cmat[pl.ds(pl.multiple_of(t * 256 + 128, 32), 32), :] = jnp.where(zlane8 == 3, w[2], 0.0).astype(BF16)
        return carry

    lax.fori_loop(0, FIRST_BANDS, band, 0)
    load_x.wait()
    def rows_of(chip, c):
        return pl.ds(pl.multiple_of(chip * 128 + SHARE[c][0], 16), SHARE[c][1])

    def aims(j, c):
        return rows_of(lax.rem(yc + j, ny), c)

    order = [(ch, j) for ch in range(nch) for j in (2, 1, 3)] + [(ch, 0) for ch in range(nch)]

    def c_copy(ch, j, owner):
        return remote(cbuf.at[ch, aims(j, owner)], cland.at[ch, aims(j, owner)], c_send.at[ch, j], c_recv.at[ch, j], sib)

    def r_copy(ch, j, c):
        return remote(
            cbuf.at[ch, aims(j, c)], rland.at[ch, j - 1, pl.ds(*SHARE[c])],
            r_send.at[ch, j - 1], r_recv.at[ch, j - 1], ychip(j),
        )

    def a_copy(ch, j, c):
        block = mixed.at[ch, aims(0, c)]
        return remote(block, block, a_send.at[ch, j - 1], a_recv.at[ch, j - 1], ychip(j))

    def f_copy(ch, j, c):
        block = mixed.at[ch, aims(ny - j, c)]
        return remote(block, block, f_send.at[ch, j], f_recv.at[ch, j], sib)

    value = dot(amat[...], fs[1, 1:129].reshape(1024, 512))
    for ch in range(nch):
        part[ch] = value[:, ch * lc : (ch + 1) * lc]
    pl.semaphore_wait(barrier, waits)

    def send_sums(c):
        for ch, j in order:
            cbuf[ch, aims(j, 1 - c), :] = part[ch, aims(j, 1 - c), :].astype(BF16)
            c_copy(ch, j, 1 - c).start()

    def answer(k):
        there, first, dev, lands = pairs[k]

        @pl.when(there & ~first)
        def _():
            pl.semaphore_signal(ready.at[lands], inc=1, device_id=dev, device_id_type=MESH)

    answer(1)
    for c in range(2):
        pl.when(core == c)(functools.partial(send_sums, c))
    answer(0)

    x_copies = [
        remote(fs.at[1, pl.ds(127, 2)], xland.at[0], x_send.at[0], x_recv.at[0], (right, h)),
        remote(fs.at[1, pl.ds(1, 2)], xland.at[1], x_send.at[1], x_recv.at[1], (left, h)),
    ]
    for copy in x_copies:
        copy.start()
    def pass_sums(c):
        for ch, j in order:
            c_copy(ch, j, c).wait_recv()
            if j > 0:
                total = part[ch, aims(j, c), :] + cland[ch, aims(j, c), :].astype(F32)
                cbuf[ch, aims(j, c), :] = total.astype(BF16)
                r_copy(ch, j, c).start()

    for c in range(2):
        pl.when(core == c)(functools.partial(pass_sums, c))

    row = lax.broadcasted_iota(jnp.int32, (64, 256), 0)
    col = lax.broadcasted_iota(jnp.int32, (64, 256), 1)
    pick = jnp.where(col == (row & 31) * 8 + jnp.where(row < 32, 7, 0), 1.0, 0.0).astype(BF16)
    for b in range(4):
        cells = fs[1, 1 + 32 * b : 33 + 32 * b].reshape(256, 512)
        picked = dot(pick, cells).astype(BF16)
        ybuf[0, 32 * b : 32 * b + 32, :] = picked[:32]
        ybuf[1, 32 * b : 32 * b + 32, :] = picked[32:]
    y_copies = [
        remote(ybuf.at[1], yland.at[1], y_send.at[1], y_recv.at[1], (g, prev)),
        remote(ybuf.at[0], yland.at[0], y_send.at[0], y_recv.at[0], (g, nxt)),
    ]
    k_copies = [
        remote(xland, cornl.at[1], k_send.at[1], k_recv.at[1], (g, prev)),
        remote(xland, cornl.at[0], k_send.at[0], k_recv.at[0], (g, nxt)),
    ]
    for (there, first, _, _), copy in zip(pairs, y_copies):
        pl.when(there & ~first)(copy.start)

    load_s.wait()

    def modes_of(c):
        return range(SHARE[c][0] // 16, (SHARE[c][0] + SHARE[c][1]) // 16)

    def mixing_weights(c):
        rep4 = jnp.where(
            (lax.broadcasted_iota(jnp.int32, (32, 128), 1) & 31) == lax.broadcasted_iota(jnp.int32, (32, 128), 0), 1.0, 0.0
        ).astype(BF16)
        sv = dot(sw[...].reshape(512, 32), rep4)
        zlane = lax.broadcasted_iota(jnp.int32, (32, 128), 1) // 32
        for m in modes_of(c):
            wr = sv[m * 64 : m * 64 + 32]
            wi = sv[m * 64 + 32 : m * 64 + 64]
            for r in range(2):
                for z in range(4):
                    first = jnp.where(zlane == z, wr if r == 0 else -wi, 0.0)
                    second = jnp.where(zlane == z, wi if r == 0 else wr, 0.0)
                    rmat[m, r * 128 + z * 32 : r * 128 + z * 32 + 32, :] = jnp.concatenate([first, second], axis=1).astype(BF16)

    for c in range(2):
        pl.when(core == c)(functools.partial(mixing_weights, c))

    lax.fori_loop(FIRST_BANDS, 9, band, 0)

    def shift(first, count):
        cells = fs[1, pl.ds(first, count)].astype(F32)
        sub = lax.broadcasted_iota(jnp.int32, cells.shape, 1)
        fs[0, pl.ds(first, count)] = jnp.where(sub == 0, 0.0, pltpu.roll(cells, 1, 1)).astype(BF16)
        fs[2, pl.ds(first, count)] = jnp.where(sub == 7, 0.0, pltpu.roll(cells, 7, 1)).astype(BF16)

    def shift_block(b, carry):
        shift(1 + b * 32, 32)
        return carry

    for copy in x_copies:
        copy.wait()
    has_left = jnp.where(g > 0, 1.0, 0.0)
    has_right = jnp.where(g < ng - 1, 1.0, 0.0)
    for (there, first, _, _), copy in zip(pairs, k_copies):
        pl.when(there & ~first)(copy.start)

    def greet_later(far):
        k = 0 if far else 1
        there, first, _, _ = pairs[k]

        @pl.when(there & first)
        def _():
            pl.semaphore_wait(ready.at[k], 1)
            y_copies[k].start()
            k_copies[k].start()

    lax.fori_loop(0, 4, shift_block, 0)
    greet_later(False)
    fs[1, 0:1] = (xland[0, 1:2].astype(F32) * has_left).astype(BF16)
    fs[1, 129:130] = (xland[1, 0:1].astype(F32) * has_right).astype(BF16)
    shift(0, 1)
    shift(129, 1)

    load_b.wait()
    bias_row = jnp.concatenate([bv[...]] * 16, axis=1)

    def windows(taps, first, count):
        low = jnp.concatenate([t[:, :256] for t in taps], axis=1)
        high = jnp.concatenate([t[:, 256:] for t in taps], axis=1)
        mid = jnp.concatenate([t[:, 128:384] for t in taps], axis=1)
        rows = low.shape[0]
        main = dot(jnp.concatenate([low, high], axis=0), tmat[first : first + count, :])
        cross = dot(mid, cmat[first : first + count, :])
        return jnp.concatenate(
            [
                main[:rows, :128], main[:rows, 128:] + cross[:, :128],
                main[rows:, :128] + cross[:, 128:], main[rows:, 128:],
            ],
            axis=1,
        )

    def conv_block(b, carry):
        taps = [fs[dy, pl.ds(b * 32 + dx, 32)].reshape(256, 512) for dy in range(3) for dx in range(3)]
        value = windows(taps, 0, 2304) + bias_row
        for t in range(4):
            conv[t, pl.ds(pl.multiple_of(b * 256, 256), 256), :] = value[:, 128 * t : 128 * t + 128]
        return carry

    lax.fori_loop(0, 2, conv_block, 0, unroll=True)

    def mix_modes(c):
        first, count = SHARE[c]
        for ch in range(nch):
            coef = part[ch, aims(0, c), :] + cland[ch, aims(0, c), :].astype(F32)
            for j in range(1, ny):
                r_copy(ch, j, c).wait_recv()
                coef = coef + rland[ch, j - 1, first : first + count, :].astype(F32)
            pieces = []
            for m in modes_of(c):
                at = m * 16 - first
                rows = jnp.concatenate(
                    [
                        jnp.concatenate(
                            [coef[at + 8 * r : at + 8 * r + 8, 128 * t : 128 * t + 128] for r in range(2)], axis=1
                        )
                        for t in range(tiles)
                    ],
                    axis=0,
                ).astype(BF16)
                mix = dot(rows, rmat[m])
                for r in range(2):
                    pieces.append(
                        jnp.concatenate([mix[8 * t : 8 * t + 8, 128 * r : 128 * r + 128] for t in range(tiles)], axis=1)
                    )
            mixed[ch, aims(0, c), :] = jnp.concatenate(pieces, axis=0).astype(BF16)
            for k in FAR_FIRST:
                a_copy(ch, k + 1, c).start()
            f_copy(ch, 0, c).start()

    for c in range(2):
        pl.when(core == c)(functools.partial(mix_modes, c))

    conv_block(2, 0)
    greet_later(True)
    conv_block(3, 0)

    row = lax.broadcasted_iota(jnp.int32, (256, 160), 0)
    col = lax.broadcasted_iota(jnp.int32, (256, 160), 1)
    x = row & 127
    def halo(side, here):
        @pl.when(pairs[side][0] & here)
        def _():
            y_copies[1 - side].wait_recv()
            k_copies[1 - side].wait_recv()
            yrow = 7 if side == 0 else 0
            inside = jnp.where(row < 128, x - 1, x + 1)
            picks = jnp.where((col == inside) & (col < 128), 1.0, 0.0)
            picks = jnp.where((row == 0) & (col == 128 + 8 + yrow), has_left, picks)
            picks = jnp.where((row == 255) & (col == 128 + 16 + yrow), has_right, picks)
            mid_rows = yland[side]
            source = jnp.concatenate([mid_rows, cornl[side].reshape(32, 512)], axis=0)
            moved = dot(picks.astype(BF16), source).astype(BF16)
            value = windows([moved[:128], mid_rows, moved[128:]], 1536 * side, 768)
            edge = pl.ds(0 if side == 0 else 7, 128, stride=8)
            for t in range(4):
                conv[t, edge, :] = conv[t, edge, :] + value[:, 128 * t : 128 * t + 128]

    far_first = lax.rem(h, 8) == 0
    halo(1, h >= 0)
    halo(0, ~far_first)

    def pass_mixed(c):
        for ch in range(nch):
            for j in (1, 3, 2):
                a_copy(ch, j, c).wait_recv()
                f_copy(ch, j, c).start()

    for c in range(2):
        pl.when(core == c)(functools.partial(pass_mixed, c))

    halo(0, far_first)

    load_i.wait()
    for ch in range(nch):

        def wait_mixed(c, ch=ch):
            for j in range(ny):
                f_copy(ch, j, 1 - c).wait_recv()

        for c in range(2):
            pl.when(core == c)(functools.partial(wait_mixed, c))

        def finish(b, carry):
            rows = pl.ds(pl.multiple_of(b * 256, 256), 256)
            lanes = slice(ch * lc, (ch + 1) * lc)
            base = jnp.concatenate([conv[ch * tiles + t, rows, :] for t in range(tiles)], axis=1)
            value = dot(gmat[rows, :], mixed[ch]) + base
            value = 0.5 * value * (1.0 + lax.erf(value * (0.5**0.5)))
            out[pl.ds(b * 32, 32), :, lanes] = value.reshape(32, 8, lc).astype(BF16)
            return carry

        lax.fori_loop(0, 4, finish, 0, unroll=True)

    def wait_sends(c):
        for ch in range(nch):
            for j in range(ny):
                c_copy(ch, j, 1 - c).wait_send()
                f_copy(ch, j, c).wait_send()
            for j in range(1, ny):
                r_copy(ch, j, c).wait_send()
                a_copy(ch, j, c).wait_send()

    for c in range(2):
        pl.when(core == c)(functools.partial(wait_sends, c))

    for (there, _, _, _), y_copy, k_copy in zip(pairs, y_copies, k_copies):

        @pl.when(there)
        def _(y_copy=y_copy, k_copy=k_copy):
            y_copy.wait_send()
            k_copy.wait_send()


def shards(field, conv_weight, conv_bias, spectral_weight):
    cells_x, cells_y, width = field.shape
    groups = lax.axis_size("gx")
    modes = spectral_weight.shape[0]
    ny = groups // 2
    lc = width // CHUNKS
    ftab, itab = expanded_tables(cells_x * groups, modes, groups, cells_y)
    dma = pltpu.SemaphoreType.DMA
    vmem = pltpu.VMEM
    scratch = [
        vmem((3, cells_x + 2, cells_y, width), BF16),
        vmem((64, 1024), BF16),
        vmem((27, 32, 32), BF16),
        vmem((8, 2, 32, 32), BF16),
        vmem((1, 32), F32),
        vmem((512, 1024), BF16),
        vmem((1024, 512), BF16),
        vmem((864, 256), F32),
        vmem((2304, 256), BF16),
        vmem((2304, 256), BF16),
        vmem((8, 256, 256), BF16),
        vmem((4, 1024, 128), F32),
        vmem((CHUNKS, 512, lc), F32),
        vmem((CHUNKS, 512, lc), BF16),
        vmem((CHUNKS, 512, lc), BF16),
        vmem((CHUNKS, ny - 1, 128, lc), BF16),
        vmem((CHUNKS, 512, lc), BF16),
        vmem((2, 128, 512), BF16),
        vmem((2, 128, 512), BF16),
        vmem((2, 2, 8, 512), BF16),
        vmem((2, 2, 2, 8, 512), BF16),
        dma((6,)), dma((1,)),
        dma((CHUNKS, ny)), dma((CHUNKS, ny)),
        dma((CHUNKS, ny - 1)), dma((CHUNKS, ny - 1)),
        dma((CHUNKS, ny - 1)), dma((CHUNKS, ny - 1)),
        dma((CHUNKS, ny)), dma((CHUNKS, ny)),
        dma((2,)), dma((2,)), dma((2,)), dma((2,)), dma((2,)), dma((2,)),
        pltpu.SemaphoreType.REGULAR((2,)),
    ]
    operands = (field, conv_weight, conv_bias.reshape(1, -1), spectral_weight, ftab, itab)
    in_hbm = pl.BlockSpec(memory_space=pltpu.HBM)
    return pl.pallas_call(
        layer_kernel,
        out_shape=jax.ShapeDtypeStruct(field.shape, BF16),
        in_specs=[in_hbm] * 6,
        out_specs=pl.BlockSpec(memory_space=pltpu.VMEM),
        scratch_shapes=scratch,
        compiler_params=pltpu.CompilerParams(
            collective_id=0, has_side_effects=True, vmem_limit_bytes=40 * 1024 * 1024
        ),
        name="layer",
    )(*(pltpu.with_memory_space_constraint(a, pltpu.HBM) for a in operands))


def solution(mesh):
    placed = (P("gx", "gy", None), P(), P(), P())
    return jax.shard_map(
        shards, mesh=mesh, in_specs=placed, out_specs=P("gx", "gy", None), check_vma=False
    )
```

```python
import functools
import math

import jax
import jax.numpy as jnp
import numpy as np
from jax import lax
from jax.experimental import pallas as pl
from jax.experimental.pallas import tpu as pltpu
from jax.sharding import PartitionSpec as P

MESH = pl.DeviceIdType.MESH
CHUNKS = 2
SPLIT_ROW = 96
FIRST_BANDS = 0
SHARE = ((SPLIT_ROW, 128 - SPLIT_ROW), (0, SPLIT_ROW))
FAR_FIRST = (1, 0, 2)
F32 = jnp.float32
BF16 = jnp.bfloat16


def dot(a, b):
    return jnp.dot(a, b, preferred_element_type=F32)


def expanded_tables(length, modes, groups, rows_y):
    turns = (np.arange(modes)[:, None] * np.arange(length)[None, :]) % length
    angles = turns.astype(np.float32) * np.float32(2.0 * math.pi / length)
    pairs = np.stack([np.cos(angles), -np.sin(angles)], axis=1) * np.float32(1.0 / math.sqrt(length))
    doubling = np.where(np.arange(modes) == 0, 1.0, 2.0).astype(np.float32)
    forward = pairs.reshape(2 * modes, groups, length // groups).transpose(1, 0, 2)
    inverse = (pairs * doubling[:, None, None]).reshape(2 * modes, groups, length // groups).transpose(1, 2, 0)
    forward = np.repeat(forward, rows_y, axis=2)
    inverse = np.kron(inverse, np.eye(rows_y, dtype=np.float32))
    return jnp.asarray(forward, BF16), jnp.asarray(inverse, BF16)


def spread(table_ref, out_ref):
    rows, lanes = table_ref.shape

    def body(i, carry):
        part = table_ref[pl.ds(pl.multiple_of(i * 16, 16), 16), :].astype(F32)
        wide = jnp.broadcast_to(part[:, None, :], (16, 8, lanes))
        keep = lax.broadcasted_iota(jnp.int32, (16, 8, lanes), 1) == (
            lax.broadcasted_iota(jnp.int32, (16, 8, lanes), 2) & 7
        )
        out_ref[pl.ds(pl.multiple_of(i * 128, 128), 128), :] = (
            jnp.where(keep, wide, 0.0).reshape(128, lanes).astype(BF16)
        )
        return carry

    lax.fori_loop(0, rows // 16, body, 0)


def layer_kernel(
    field, convw, bias, specw, ftab, itab, out,
    fs, fexp, cw, sw, bv, amat, gmat, wrep, tmat, cmat, rmat, conv,
    part, cbuf, cland, rland, mixed, ybuf, yland, xland, cornl,
    load_sem, bar_send, c_send, c_recv, r_send, r_recv, a_send, a_recv, f_send, f_recv,
    x_send, x_recv, y_send, y_recv, k_send, k_recv, ready,
):
    nch, _, lc = mixed.shape
    tiles = lc // 128
    g = lax.axis_index("gx")
    h = lax.axis_index("gy")
    ng = lax.axis_size("gx")
    nh = lax.axis_size("gy")
    ny = ng // 2
    yc, core = g // 2, g % 2
    sib = (2 * yc + (1 - core), h)

    def ychip(j):
        return (2 * lax.rem(yc + j, ny) + core, h)

    left, right = lax.rem(g + ng - 1, ng), lax.rem(g + 1, ng)
    prev, nxt = lax.rem(h + nh - 1, nh), lax.rem(h + 1, nh)
    outer = lax.rem(g + ng + 2 * core - 1, ng)

    def remote(src, dst, s, r, dev):
        return pltpu.make_async_remote_copy(
            src_ref=src, dst_ref=dst, send_sem=s, recv_sem=r, device_id=dev, device_id_type=MESH
        )

    load_f = pltpu.make_async_copy(ftab.at[g], fexp, load_sem.at[0])
    load_x = pltpu.make_async_copy(field, fs.at[1, pl.ds(1, 128)], load_sem.at[1])
    load_i = pltpu.make_async_copy(itab.at[g], gmat, load_sem.at[2])
    load_w = pltpu.make_async_copy(convw, cw, load_sem.at[3])
    load_s = pltpu.make_async_copy(specw.at[pl.ds(8 * yc, 8)], sw, load_sem.at[4])
    load_b = pltpu.make_async_copy(bias, bv, load_sem.at[5])
    for load in (load_f, load_x, load_w, load_s, load_b, load_i):
        load.start()

    barrier = pltpu.get_barrier_semaphore()
    chips = [ychip(j) for j in range(1, ny)]
    for dev in [sib, (outer, h)] + chips:
        pl.semaphore_signal(barrier, inc=1, device_id=dev, device_id_type=MESH)
    first_up = lax.rem(h + 1, 8) != 0
    first_down = lax.rem(h, 8) == 0
    has_up, has_down = h < nh - 1, h > 0
    pairs = [
        (has_down, first_down, (g, prev), 1),
        (has_up, first_up, (g, nxt), 0),
    ]
    waits = jnp.int32(2 + len(chips))
    for there, first, dev, _ in pairs:

        @pl.when(there & first)
        def _(dev=dev):
            pl.semaphore_signal(barrier, inc=1, device_id=dev, device_id_type=MESH)

        waits = waits + jnp.where(there & ~first, 1, 0)

    load_f.wait()
    spread(fexp, amat)
    load_w.wait()
    rep8 = jnp.where(
        (lax.broadcasted_iota(jnp.int32, (32, 256), 1) & 31) == lax.broadcasted_iota(jnp.int32, (32, 256), 0), 1.0, 0.0
    ).astype(BF16)
    wrep[...] = dot(cw[...].reshape(864, 32), rep8)
    zlane8 = lax.broadcasted_iota(jnp.int32, (32, 256), 1) // 32
    cmat[...] = jnp.zeros_like(cmat)

    def band(t, carry):
        dyi, dxi = t // 3, t % 3
        base = pl.multiple_of((dxi * 3 + dyi) * 96, 32)
        w = [wrep[pl.ds(pl.multiple_of(base + 32 * k, 32), 32), :] for k in range(3)]
        for z in range(8):
            block = jnp.where(zlane8 == z + 1, w[0], 0.0)
            block = jnp.where(zlane8 == z, w[1], block)
            block = jnp.where(zlane8 == z - 1, w[2], block)
            tmat[pl.ds(pl.multiple_of(t * 256 + z * 32, 32), 32), :] = block.astype(BF16)
        cmat[pl.ds(pl.multiple_of(t * 256 + 96, 32), 32), :] = jnp.where(zlane8 == 4, w[0], 0.0).astype(BF16)
        cmat[pl.ds(pl.multiple_of(t * 256 + 128, 32), 32), :] = jnp.where(zlane8 == 3, w[2], 0.0).astype(BF16)
        return carry

    lax.fori_loop(0, FIRST_BANDS, band, 0)
    load_x.wait()
    def rows_of(chip, c):
        return pl.ds(pl.multiple_of(chip * 128 + SHARE[c][0], 16), SHARE[c][1])

    def aims(j, c):
        return rows_of(lax.rem(yc + j, ny), c)

    order = [(ch, j) for ch in range(nch) for j in (2, 1, 3)] + [(ch, 0) for ch in range(nch)]

    def c_copy(ch, j, owner):
        return remote(cbuf.at[ch, aims(j, owner)], cland.at[ch, aims(j, owner)], c_send.at[ch, j], c_recv.at[ch, j], sib)

    def r_copy(ch, j, c):
        return remote(
            cbuf.at[ch, aims(j, c)], rland.at[ch, j - 1, pl.ds(*SHARE[c])],
            r_send.at[ch, j - 1], r_recv.at[ch, j - 1], ychip(j),
        )

    def a_copy(ch, j, c):
        block = mixed.at[ch, aims(0, c)]
        return remote(block, block, a_send.at[ch, j - 1], a_recv.at[ch, j - 1], ychip(j))

    def f_copy(ch, j, c):
        block = mixed.at[ch, aims(ny - j, c)]
        return remote(block, block, f_send.at[ch, j], f_recv.at[ch, j], sib)

    value = dot(amat[...], fs[1, 1:129].reshape(1024, 512))
    for ch in range(nch):
        part[ch] = value[:, ch * lc : (ch + 1) * lc]
    pl.semaphore_wait(barrier, waits)

    def send_sums(c):
        for ch, j in order:
            cbuf[ch, aims(j, 1 - c), :] = part[ch, aims(j, 1 - c), :].astype(BF16)
            c_copy(ch, j, 1 - c).start()

    for c in range(2):
        pl.when(core == c)(functools.partial(send_sums, c))

    for there, first, dev, lands in pairs:

        @pl.when(there & ~first)
        def _(dev=dev, lands=lands):
            pl.semaphore_signal(ready.at[lands], inc=1, device_id=dev, device_id_type=MESH)

    x_copies = [
        remote(fs.at[1, pl.ds(127, 2)], xland.at[0], x_send.at[0], x_recv.at[0], (right, h)),
        remote(fs.at[1, pl.ds(1, 2)], xland.at[1], x_send.at[1], x_recv.at[1], (left, h)),
    ]
    for copy in x_copies:
        copy.start()
    row = lax.broadcasted_iota(jnp.int32, (64, 256), 0)
    col = lax.broadcasted_iota(jnp.int32, (64, 256), 1)
    pick = jnp.where(col == (row & 31) * 8 + jnp.where(row < 32, 7, 0), 1.0, 0.0).astype(BF16)
    for b in range(4):
        cells = fs[1, 1 + 32 * b : 33 + 32 * b].reshape(256, 512)
        picked = dot(pick, cells).astype(BF16)
        ybuf[0, 32 * b : 32 * b + 32, :] = picked[:32]
        ybuf[1, 32 * b : 32 * b + 32, :] = picked[32:]
    y_copies = [
        remote(ybuf.at[1], yland.at[1], y_send.at[1], y_recv.at[1], (g, prev)),
        remote(ybuf.at[0], yland.at[0], y_send.at[0], y_recv.at[0], (g, nxt)),
    ]
    k_copies = [
        remote(xland, cornl.at[1], k_send.at[1], k_recv.at[1], (g, prev)),
        remote(xland, cornl.at[0], k_send.at[0], k_recv.at[0], (g, nxt)),
    ]
    for (there, first, _, _), copy in zip(pairs, y_copies):
        pl.when(there & ~first)(copy.start)

    def pass_sums(c):
        for ch, j in order:
            c_copy(ch, j, c).wait_recv()
            if j > 0:
                total = part[ch, aims(j, c), :] + cland[ch, aims(j, c), :].astype(F32)
                cbuf[ch, aims(j, c), :] = total.astype(BF16)
                r_copy(ch, j, c).start()

    for c in range(2):
        pl.when(core == c)(functools.partial(pass_sums, c))

    load_s.wait()

    def modes_of(c):
        return range(SHARE[c][0] // 16, (SHARE[c][0] + SHARE[c][1]) // 16)

    def mixing_weights(c):
        rep4 = jnp.where(
            (lax.broadcasted_iota(jnp.int32, (32, 128), 1) & 31) == lax.broadcasted_iota(jnp.int32, (32, 128), 0), 1.0, 0.0
        ).astype(BF16)
        sv = dot(sw[...].reshape(512, 32), rep4)
        zlane = lax.broadcasted_iota(jnp.int32, (32, 128), 1) // 32
        for m in modes_of(c):
            wr = sv[m * 64 : m * 64 + 32]
            wi = sv[m * 64 + 32 : m * 64 + 64]
            for r in range(2):
                for z in range(4):
                    first = jnp.where(zlane == z, wr if r == 0 else -wi, 0.0)
                    second = jnp.where(zlane == z, wi if r == 0 else wr, 0.0)
                    rmat[m, r * 128 + z * 32 : r * 128 + z * 32 + 32, :] = jnp.concatenate([first, second], axis=1).astype(BF16)

    for c in range(2):
        pl.when(core == c)(functools.partial(mixing_weights, c))

    lax.fori_loop(FIRST_BANDS, 9, band, 0)

    def shift(first, count):
        cells = fs[1, pl.ds(first, count)].astype(F32)
        sub = lax.broadcasted_iota(jnp.int32, cells.shape, 1)
        fs[0, pl.ds(first, count)] = jnp.where(sub == 0, 0.0, pltpu.roll(cells, 1, 1)).astype(BF16)
        fs[2, pl.ds(first, count)] = jnp.where(sub == 7, 0.0, pltpu.roll(cells, 7, 1)).astype(BF16)

    def shift_block(b, carry):
        shift(1 + b * 32, 32)
        return carry

    lax.fori_loop(0, 4, shift_block, 0)
    for copy in x_copies:
        copy.wait()
    has_left = jnp.where(g > 0, 1.0, 0.0)
    has_right = jnp.where(g < ng - 1, 1.0, 0.0)
    for (there, first, _, _), copy in zip(pairs, k_copies):
        pl.when(there & ~first)(copy.start)

    def greet_later(far):
        k = 0 if far else 1
        there, first, _, _ = pairs[k]

        @pl.when(there & first)
        def _():
            pl.semaphore_wait(ready.at[k], 1)
            y_copies[k].start()
            k_copies[k].start()

    greet_later(False)
    fs[1, 0:1] = (xland[0, 1:2].astype(F32) * has_left).astype(BF16)
    fs[1, 129:130] = (xland[1, 0:1].astype(F32) * has_right).astype(BF16)
    shift(0, 1)
    shift(129, 1)

    load_b.wait()
    bias_row = jnp.concatenate([bv[...]] * 16, axis=1)

    def windows(taps, first, count):
        low = jnp.concatenate([t[:, :256] for t in taps], axis=1)
        high = jnp.concatenate([t[:, 256:] for t in taps], axis=1)
        mid = jnp.concatenate([t[:, 128:384] for t in taps], axis=1)
        rows = low.shape[0]
        main = dot(jnp.concatenate([low, high], axis=0), tmat[first : first + count, :])
        cross = dot(mid, cmat[first : first + count, :])
        return jnp.concatenate(
            [
                main[:rows, :128], main[:rows, 128:] + cross[:, :128],
                main[rows:, :128] + cross[:, 128:], main[rows:, 128:],
            ],
            axis=1,
        )

    def conv_block(b, carry):
        taps = [fs[dy, pl.ds(b * 32 + dx, 32)].reshape(256, 512) for dy in range(3) for dx in range(3)]
        value = windows(taps, 0, 2304) + bias_row
        for t in range(4):
            conv[t, pl.ds(pl.multiple_of(b * 256, 256), 256), :] = value[:, 128 * t : 128 * t + 128]
        return carry

    lax.fori_loop(0, 2, conv_block, 0, unroll=True)

    def mix_modes(c):
        first, count = SHARE[c]
        for ch in range(nch):
            coef = part[ch, aims(0, c), :] + cland[ch, aims(0, c), :].astype(F32)
            for j in range(1, ny):
                r_copy(ch, j, c).wait_recv()
                coef = coef + rland[ch, j - 1, first : first + count, :].astype(F32)
            pieces = []
            for m in modes_of(c):
                at = m * 16 - first
                rows = jnp.concatenate(
                    [
                        jnp.concatenate(
                            [coef[at + 8 * r : at + 8 * r + 8, 128 * t : 128 * t + 128] for r in range(2)], axis=1
                        )
                        for t in range(tiles)
                    ],
                    axis=0,
                ).astype(BF16)
                mix = dot(rows, rmat[m])
                for r in range(2):
                    pieces.append(
                        jnp.concatenate([mix[8 * t : 8 * t + 8, 128 * r : 128 * r + 128] for t in range(tiles)], axis=1)
                    )
            mixed[ch, aims(0, c), :] = jnp.concatenate(pieces, axis=0).astype(BF16)
            for k in FAR_FIRST:
                a_copy(ch, k + 1, c).start()
            f_copy(ch, 0, c).start()

    for c in range(2):
        pl.when(core == c)(functools.partial(mix_modes, c))

    greet_later(True)

    lax.fori_loop(2, 4, conv_block, 0, unroll=True)

    row = lax.broadcasted_iota(jnp.int32, (256, 160), 0)
    col = lax.broadcasted_iota(jnp.int32, (256, 160), 1)
    x = row & 127
    def halo(side, here):
        @pl.when(pairs[side][0] & here)
        def _():
            y_copies[1 - side].wait_recv()
            k_copies[1 - side].wait_recv()
            yrow = 7 if side == 0 else 0
            inside = jnp.where(row < 128, x - 1, x + 1)
            picks = jnp.where((col == inside) & (col < 128), 1.0, 0.0)
            picks = jnp.where((row == 0) & (col == 128 + 8 + yrow), has_left, picks)
            picks = jnp.where((row == 255) & (col == 128 + 16 + yrow), has_right, picks)
            mid_rows = yland[side]
            source = jnp.concatenate([mid_rows, cornl[side].reshape(32, 512)], axis=0)
            moved = dot(picks.astype(BF16), source).astype(BF16)
            value = windows([moved[:128], mid_rows, moved[128:]], 1536 * side, 768)
            edge = pl.ds(0 if side == 0 else 7, 128, stride=8)
            for t in range(4):
                conv[t, edge, :] = conv[t, edge, :] + value[:, 128 * t : 128 * t + 128]

    far_first = lax.rem(h, 8) == 0
    halo(1, h >= 0)
    halo(0, ~far_first)

    def pass_mixed(c):
        for ch in range(nch):
            for j in (1, 3, 2):
                a_copy(ch, j, c).wait_recv()
                f_copy(ch, j, c).start()

    for c in range(2):
        pl.when(core == c)(functools.partial(pass_mixed, c))

    halo(0, far_first)

    load_i.wait()
    for ch in range(nch):

        def wait_mixed(c, ch=ch):
            for j in range(ny):
                f_copy(ch, j, 1 - c).wait_recv()

        for c in range(2):
            pl.when(core == c)(functools.partial(wait_mixed, c))

        def finish(b, carry):
            rows = pl.ds(pl.multiple_of(b * 256, 256), 256)
            lanes = slice(ch * lc, (ch + 1) * lc)
            base = jnp.concatenate([conv[ch * tiles + t, rows, :] for t in range(tiles)], axis=1)
            value = dot(gmat[rows, :], mixed[ch]) + base
            value = 0.5 * value * (1.0 + lax.erf(value * (0.5**0.5)))
            out[pl.ds(b * 32, 32), :, lanes] = value.reshape(32, 8, lc).astype(BF16)
            return carry

        lax.fori_loop(0, 4, finish, 0, unroll=True)

    def wait_sends(c):
        for ch in range(nch):
            for j in range(ny):
                c_copy(ch, j, 1 - c).wait_send()
                f_copy(ch, j, c).wait_send()
            for j in range(1, ny):
                r_copy(ch, j, c).wait_send()
                a_copy(ch, j, c).wait_send()

    for c in range(2):
        pl.when(core == c)(functools.partial(wait_sends, c))

    for (there, _, _, _), y_copy, k_copy in zip(pairs, y_copies, k_copies):

        @pl.when(there)
        def _(y_copy=y_copy, k_copy=k_copy):
            y_copy.wait_send()
            k_copy.wait_send()


def shards(field, conv_weight, conv_bias, spectral_weight):
    cells_x, cells_y, width = field.shape
    groups = lax.axis_size("gx")
    modes = spectral_weight.shape[0]
    ny = groups // 2
    lc = width // CHUNKS
    ftab, itab = expanded_tables(cells_x * groups, modes, groups, cells_y)
    dma = pltpu.SemaphoreType.DMA
    vmem = pltpu.VMEM
    scratch = [
        vmem((3, cells_x + 2, cells_y, width), BF16),
        vmem((64, 1024), BF16),
        vmem((27, 32, 32), BF16),
        vmem((8, 2, 32, 32), BF16),
        vmem((1, 32), F32),
        vmem((512, 1024), BF16),
        vmem((1024, 512), BF16),
        vmem((864, 256), F32),
        vmem((2304, 256), BF16),
        vmem((2304, 256), BF16),
        vmem((8, 256, 256), BF16),
        vmem((4, 1024, 128), F32),
        vmem((CHUNKS, 512, lc), F32),
        vmem((CHUNKS, 512, lc), BF16),
        vmem((CHUNKS, 512, lc), BF16),
        vmem((CHUNKS, ny - 1, 128, lc), BF16),
        vmem((CHUNKS, 512, lc), BF16),
        vmem((2, 128, 512), BF16),
        vmem((2, 128, 512), BF16),
        vmem((2, 2, 8, 512), BF16),
        vmem((2, 2, 2, 8, 512), BF16),
        dma((6,)), dma((1,)),
        dma((CHUNKS, ny)), dma((CHUNKS, ny)),
        dma((CHUNKS, ny - 1)), dma((CHUNKS, ny - 1)),
        dma((CHUNKS, ny - 1)), dma((CHUNKS, ny - 1)),
        dma((CHUNKS, ny)), dma((CHUNKS, ny)),
        dma((2,)), dma((2,)), dma((2,)), dma((2,)), dma((2,)), dma((2,)),
        pltpu.SemaphoreType.REGULAR((2,)),
    ]
    operands = (field, conv_weight, conv_bias.reshape(1, -1), spectral_weight, ftab, itab)
    in_hbm = pl.BlockSpec(memory_space=pltpu.HBM)
    return pl.pallas_call(
        layer_kernel,
        out_shape=jax.ShapeDtypeStruct(field.shape, BF16),
        in_specs=[in_hbm] * 6,
        out_specs=pl.BlockSpec(memory_space=pltpu.VMEM),
        scratch_shapes=scratch,
        compiler_params=pltpu.CompilerParams(
            collective_id=0, has_side_effects=True, vmem_limit_bytes=40 * 1024 * 1024
        ),
        name="layer",
    )(*(pltpu.with_memory_space_constraint(a, pltpu.HBM) for a in operands))


def solution(mesh):
    placed = (P("gx", "gy", None), P(), P(), P())
    return jax.shard_map(
        shards, mesh=mesh, in_specs=placed, out_specs=P("gx", "gy", None), check_vma=False
    )
```

```python
import functools
import math

import jax
import jax.numpy as jnp
import numpy as np
from jax import lax
from jax.experimental import pallas as pl
from jax.experimental.pallas import tpu as pltpu
from jax.sharding import PartitionSpec as P

MESH = pl.DeviceIdType.MESH
CHUNKS = 2
SPLIT_ROW = 96
FIRST_BANDS = 0
SHARE = ((SPLIT_ROW, 128 - SPLIT_ROW), (0, SPLIT_ROW))
FAR_FIRST = (1, 0, 2)
F32 = jnp.float32
BF16 = jnp.bfloat16


def dot(a, b):
    return jnp.dot(a, b, preferred_element_type=F32)


def expanded_tables(length, modes, groups, rows_y):
    turns = (np.arange(modes)[:, None] * np.arange(length)[None, :]) % length
    angles = turns.astype(np.float32) * np.float32(2.0 * math.pi / length)
    pairs = np.stack([np.cos(angles), -np.sin(angles)], axis=1) * np.float32(1.0 / math.sqrt(length))
    doubling = np.where(np.arange(modes) == 0, 1.0, 2.0).astype(np.float32)
    forward = pairs.reshape(2 * modes, groups, length // groups).transpose(1, 0, 2)
    inverse = (pairs * doubling[:, None, None]).reshape(2 * modes, groups, length // groups).transpose(1, 2, 0)
    forward = np.repeat(forward, rows_y, axis=2)
    inverse = np.kron(inverse, np.eye(rows_y, dtype=np.float32))
    return jnp.asarray(forward, BF16), jnp.asarray(inverse, BF16)


def spread(table_ref, out_ref):
    rows, lanes = table_ref.shape

    def body(i, carry):
        part = table_ref[pl.ds(pl.multiple_of(i * 16, 16), 16), :].astype(F32)
        wide = jnp.broadcast_to(part[:, None, :], (16, 8, lanes))
        keep = lax.broadcasted_iota(jnp.int32, (16, 8, lanes), 1) == (
            lax.broadcasted_iota(jnp.int32, (16, 8, lanes), 2) & 7
        )
        out_ref[pl.ds(pl.multiple_of(i * 128, 128), 128), :] = (
            jnp.where(keep, wide, 0.0).reshape(128, lanes).astype(BF16)
        )
        return carry

    lax.fori_loop(0, rows // 16, body, 0)


def layer_kernel(
    field, convw, bias, specw, ftab, itab, out,
    fs, fexp, cw, sw, bv, amat, gmat, wrep, tmat, cmat, rmat, conv,
    part, cbuf, cland, rland, mixed, ybuf, yland, xland, cornl,
    load_sem, bar_send, c_send, c_recv, r_send, r_recv, a_send, a_recv, f_send, f_recv,
    x_send, x_recv, y_send, y_recv, k_send, k_recv, ready,
):
    nch, _, lc = mixed.shape
    tiles = lc // 128
    g = lax.axis_index("gx")
    h = lax.axis_index("gy")
    ng = lax.axis_size("gx")
    nh = lax.axis_size("gy")
    ny = ng // 2
    yc, core = g // 2, g % 2
    sib = (2 * yc + (1 - core), h)

    def ychip(j):
        return (2 * lax.rem(yc + j, ny) + core, h)

    left, right = lax.rem(g + ng - 1, ng), lax.rem(g + 1, ng)
    prev, nxt = lax.rem(h + nh - 1, nh), lax.rem(h + 1, nh)
    outer = lax.rem(g + ng + 2 * core - 1, ng)

    def remote(src, dst, s, r, dev):
        return pltpu.make_async_remote_copy(
            src_ref=src, dst_ref=dst, send_sem=s, recv_sem=r, device_id=dev, device_id_type=MESH
        )

    load_f = pltpu.make_async_copy(ftab.at[g], fexp, load_sem.at[0])
    load_x = pltpu.make_async_copy(field, fs.at[1, pl.ds(1, 128)], load_sem.at[1])
    load_i = pltpu.make_async_copy(itab.at[g], gmat, load_sem.at[2])
    load_w = pltpu.make_async_copy(convw, cw, load_sem.at[3])
    load_s = pltpu.make_async_copy(specw.at[pl.ds(8 * yc, 8)], sw, load_sem.at[4])
    load_b = pltpu.make_async_copy(bias, bv, load_sem.at[5])
    for load in (load_f, load_x, load_w, load_s, load_b, load_i):
        load.start()

    barrier = pltpu.get_barrier_semaphore()
    chips = [ychip(j) for j in range(1, ny)]
    for dev in [sib, (outer, h)] + chips:
        pl.semaphore_signal(barrier, inc=1, device_id=dev, device_id_type=MESH)
    first_up = lax.rem(h + 1, 8) != 0
    first_down = lax.rem(h, 8) == 0
    has_up, has_down = h < nh - 1, h > 0
    pairs = [
        (has_down, first_down, (g, prev), 1),
        (has_up, first_up, (g, nxt), 0),
    ]
    waits = jnp.int32(2 + len(chips))
    for there, first, dev, _ in pairs:

        @pl.when(there & first)
        def _(dev=dev):
            pl.semaphore_signal(barrier, inc=1, device_id=dev, device_id_type=MESH)

        waits = waits + jnp.where(there & ~first, 1, 0)

    load_f.wait()
    spread(fexp, amat)
    load_w.wait()
    rep8 = jnp.where(
        (lax.broadcasted_iota(jnp.int32, (32, 256), 1) & 31) == lax.broadcasted_iota(jnp.int32, (32, 256), 0), 1.0, 0.0
    ).astype(BF16)
    wrep[...] = dot(cw[...].reshape(864, 32), rep8)
    zlane8 = lax.broadcasted_iota(jnp.int32, (32, 256), 1) // 32
    cmat[...] = jnp.zeros_like(cmat)

    def band(t, carry):
        dyi, dxi = t // 3, t % 3
        base = pl.multiple_of((dxi * 3 + dyi) * 96, 32)
        w = [wrep[pl.ds(pl.multiple_of(base + 32 * k, 32), 32), :] for k in range(3)]
        for z in range(8):
            block = jnp.where(zlane8 == z + 1, w[0], 0.0)
            block = jnp.where(zlane8 == z, w[1], block)
            block = jnp.where(zlane8 == z - 1, w[2], block)
            tmat[pl.ds(pl.multiple_of(t * 256 + z * 32, 32), 32), :] = block.astype(BF16)
        cmat[pl.ds(pl.multiple_of(t * 256 + 96, 32), 32), :] = jnp.where(zlane8 == 4, w[0], 0.0).astype(BF16)
        cmat[pl.ds(pl.multiple_of(t * 256 + 128, 32), 32), :] = jnp.where(zlane8 == 3, w[2], 0.0).astype(BF16)
        return carry

    lax.fori_loop(0, FIRST_BANDS, band, 0)
    load_x.wait()
    def rows_of(chip, c):
        return pl.ds(pl.multiple_of(chip * 128 + SHARE[c][0], 16), SHARE[c][1])

    def aims(j, c):
        return rows_of(lax.rem(yc + j, ny), c)

    order = [(ch, j) for ch in range(nch) for j in (2, 1, 3)] + [(ch, 0) for ch in range(nch)]

    def c_copy(ch, j, owner):
        return remote(cbuf.at[ch, aims(j, owner)], cland.at[ch, aims(j, owner)], c_send.at[ch, j], c_recv.at[ch, j], sib)

    def r_copy(ch, j, c):
        return remote(
            cbuf.at[ch, aims(j, c)], rland.at[ch, j - 1, pl.ds(*SHARE[c])],
            r_send.at[ch, j - 1], r_recv.at[ch, j - 1], ychip(j),
        )

    def a_copy(ch, j, c):
        block = mixed.at[ch, aims(0, c)]
        return remote(block, block, a_send.at[ch, j - 1], a_recv.at[ch, j - 1], ychip(j))

    def f_copy(ch, j, c):
        block = mixed.at[ch, aims(ny - j, c)]
        return remote(block, block, f_send.at[ch, j], f_recv.at[ch, j], sib)

    value = dot(amat[...], fs[1, 1:129].reshape(1024, 512))
    for ch in range(nch):
        part[ch] = value[:, ch * lc : (ch + 1) * lc]
    pl.semaphore_wait(barrier, waits)

    def send_sums(c):
        for ch, j in order:
            cbuf[ch, aims(j, 1 - c), :] = part[ch, aims(j, 1 - c), :].astype(BF16)
            c_copy(ch, j, 1 - c).start()

    for c in range(2):
        pl.when(core == c)(functools.partial(send_sums, c))

    for there, first, dev, lands in pairs:

        @pl.when(there & ~first)
        def _(dev=dev, lands=lands):
            pl.semaphore_signal(ready.at[lands], inc=1, device_id=dev, device_id_type=MESH)

    x_copies = [
        remote(fs.at[1, pl.ds(127, 2)], xland.at[0], x_send.at[0], x_recv.at[0], (right, h)),
        remote(fs.at[1, pl.ds(1, 2)], xland.at[1], x_send.at[1], x_recv.at[1], (left, h)),
    ]
    for copy in x_copies:
        copy.start()
    row = lax.broadcasted_iota(jnp.int32, (64, 256), 0)
    col = lax.broadcasted_iota(jnp.int32, (64, 256), 1)
    pick = jnp.where(col == (row & 31) * 8 + jnp.where(row < 32, 7, 0), 1.0, 0.0).astype(BF16)
    for b in range(4):
        cells = fs[1, 1 + 32 * b : 33 + 32 * b].reshape(256, 512)
        picked = dot(pick, cells).astype(BF16)
        ybuf[0, 32 * b : 32 * b + 32, :] = picked[:32]
        ybuf[1, 32 * b : 32 * b + 32, :] = picked[32:]
    y_copies = [
        remote(ybuf.at[1], yland.at[1], y_send.at[1], y_recv.at[1], (g, prev)),
        remote(ybuf.at[0], yland.at[0], y_send.at[0], y_recv.at[0], (g, nxt)),
    ]
    k_copies = [
        remote(xland, cornl.at[1], k_send.at[1], k_recv.at[1], (g, prev)),
        remote(xland, cornl.at[0], k_send.at[0], k_recv.at[0], (g, nxt)),
    ]
    for (there, first, _, _), copy in zip(pairs, y_copies):
        pl.when(there & ~first)(copy.start)

    def pass_sums(c):
        for ch, j in order:
            c_copy(ch, j, c).wait_recv()
            if j > 0:
                total = part[ch, aims(j, c), :] + cland[ch, aims(j, c), :].astype(F32)
                cbuf[ch, aims(j, c), :] = total.astype(BF16)
                r_copy(ch, j, c).start()

    for c in range(2):
        pl.when(core == c)(functools.partial(pass_sums, c))

    load_s.wait()

    def modes_of(c):
        return range(SHARE[c][0] // 16, (SHARE[c][0] + SHARE[c][1]) // 16)

    def mixing_weights(c):
        rep4 = jnp.where(
            (lax.broadcasted_iota(jnp.int32, (32, 128), 1) & 31) == lax.broadcasted_iota(jnp.int32, (32, 128), 0), 1.0, 0.0
        ).astype(BF16)
        sv = dot(sw[...].reshape(512, 32), rep4)
        zlane = lax.broadcasted_iota(jnp.int32, (32, 128), 1) // 32
        for m in modes_of(c):
            wr = sv[m * 64 : m * 64 + 32]
            wi = sv[m * 64 + 32 : m * 64 + 64]
            for r in range(2):
                for z in range(4):
                    first = jnp.where(zlane == z, wr if r == 0 else -wi, 0.0)
                    second = jnp.where(zlane == z, wi if r == 0 else wr, 0.0)
                    rmat[m, r * 128 + z * 32 : r * 128 + z * 32 + 32, :] = jnp.concatenate([first, second], axis=1).astype(BF16)

    for c in range(2):
        pl.when(core == c)(functools.partial(mixing_weights, c))

    lax.fori_loop(FIRST_BANDS, 9, band, 0)

    def shift(first, count):
        cells = fs[1, pl.ds(first, count)].astype(F32)
        sub = lax.broadcasted_iota(jnp.int32, cells.shape, 1)
        fs[0, pl.ds(first, count)] = jnp.where(sub == 0, 0.0, pltpu.roll(cells, 1, 1)).astype(BF16)
        fs[2, pl.ds(first, count)] = jnp.where(sub == 7, 0.0, pltpu.roll(cells, 7, 1)).astype(BF16)

    def shift_block(b, carry):
        shift(1 + b * 32, 32)
        return carry

    for copy in x_copies:
        copy.wait()
    has_left = jnp.where(g > 0, 1.0, 0.0)
    has_right = jnp.where(g < ng - 1, 1.0, 0.0)
    for (there, first, _, _), copy in zip(pairs, k_copies):
        pl.when(there & ~first)(copy.start)

    def greet_later(far):
        k = 0 if far else 1
        there, first, _, _ = pairs[k]

        @pl.when(there & first)
        def _():
            pl.semaphore_wait(ready.at[k], 1)
            y_copies[k].start()
            k_copies[k].start()

    lax.fori_loop(0, 4, shift_block, 0)
    greet_later(False)
    fs[1, 0:1] = (xland[0, 1:2].astype(F32) * has_left).astype(BF16)
    fs[1, 129:130] = (xland[1, 0:1].astype(F32) * has_right).astype(BF16)
    shift(0, 1)
    shift(129, 1)

    load_b.wait()
    bias_row = jnp.concatenate([bv[...]] * 16, axis=1)

    def windows(taps, first, count):
        low = jnp.concatenate([t[:, :256] for t in taps], axis=1)
        high = jnp.concatenate([t[:, 256:] for t in taps], axis=1)
        mid = jnp.concatenate([t[:, 128:384] for t in taps], axis=1)
        rows = low.shape[0]
        main = dot(jnp.concatenate([low, high], axis=0), tmat[first : first + count, :])
        cross = dot(mid, cmat[first : first + count, :])
        return jnp.concatenate(
            [
                main[:rows, :128], main[:rows, 128:] + cross[:, :128],
                main[rows:, :128] + cross[:, 128:], main[rows:, 128:],
            ],
            axis=1,
        )

    def conv_block(b, carry):
        taps = [fs[dy, pl.ds(b * 32 + dx, 32)].reshape(256, 512) for dy in range(3) for dx in range(3)]
        value = windows(taps, 0, 2304) + bias_row
        for t in range(4):
            conv[t, pl.ds(pl.multiple_of(b * 256, 256), 256), :] = value[:, 128 * t : 128 * t + 128]
        return carry

    lax.fori_loop(0, 2, conv_block, 0, unroll=True)

    def mix_modes(c):
        first, count = SHARE[c]
        for ch in range(nch):
            coef = part[ch, aims(0, c), :] + cland[ch, aims(0, c), :].astype(F32)
            for j in range(1, ny):
                r_copy(ch, j, c).wait_recv()
                coef = coef + rland[ch, j - 1, first : first + count, :].astype(F32)
            pieces = []
            for m in modes_of(c):
                at = m * 16 - first
                rows = jnp.concatenate(
                    [
                        jnp.concatenate(
                            [coef[at + 8 * r : at + 8 * r + 8, 128 * t : 128 * t + 128] for r in range(2)], axis=1
                        )
                        for t in range(tiles)
                    ],
                    axis=0,
                ).astype(BF16)
                mix = dot(rows, rmat[m])
                for r in range(2):
                    pieces.append(
                        jnp.concatenate([mix[8 * t : 8 * t + 8, 128 * r : 128 * r + 128] for t in range(tiles)], axis=1)
                    )
            mixed[ch, aims(0, c), :] = jnp.concatenate(pieces, axis=0).astype(BF16)
            for k in FAR_FIRST:
                a_copy(ch, k + 1, c).start()
            f_copy(ch, 0, c).start()

    for c in range(2):
        pl.when(core == c)(functools.partial(mix_modes, c))

    greet_later(True)

    lax.fori_loop(2, 4, conv_block, 0, unroll=True)

    row = lax.broadcasted_iota(jnp.int32, (256, 160), 0)
    col = lax.broadcasted_iota(jnp.int32, (256, 160), 1)
    x = row & 127
    def halo(side, here):
        @pl.when(pairs[side][0] & here)
        def _():
            y_copies[1 - side].wait_recv()
            k_copies[1 - side].wait_recv()
            yrow = 7 if side == 0 else 0
            inside = jnp.where(row < 128, x - 1, x + 1)
            picks = jnp.where((col == inside) & (col < 128), 1.0, 0.0)
            picks = jnp.where((row == 0) & (col == 128 + 8 + yrow), has_left, picks)
            picks = jnp.where((row == 255) & (col == 128 + 16 + yrow), has_right, picks)
            mid_rows = yland[side]
            source = jnp.concatenate([mid_rows, cornl[side].reshape(32, 512)], axis=0)
            moved = dot(picks.astype(BF16), source).astype(BF16)
            value = windows([moved[:128], mid_rows, moved[128:]], 1536 * side, 768)
            edge = pl.ds(0 if side == 0 else 7, 128, stride=8)
            for t in range(4):
                conv[t, edge, :] = conv[t, edge, :] + value[:, 128 * t : 128 * t + 128]

    far_first = lax.rem(h, 8) == 0
    halo(1, h >= 0)
    halo(0, ~far_first)

    def pass_mixed(c):
        for ch in range(nch):
            for j in (1, 3, 2):
                a_copy(ch, j, c).wait_recv()
                f_copy(ch, j, c).start()

    for c in range(2):
        pl.when(core == c)(functools.partial(pass_mixed, c))

    halo(0, far_first)

    load_i.wait()
    for ch in range(nch):

        def wait_mixed(c, ch=ch):
            for j in range(ny):
                f_copy(ch, j, 1 - c).wait_recv()

        for c in range(2):
            pl.when(core == c)(functools.partial(wait_mixed, c))

        def finish(b, carry):
            rows = pl.ds(pl.multiple_of(b * 256, 256), 256)
            lanes = slice(ch * lc, (ch + 1) * lc)
            base = jnp.concatenate([conv[ch * tiles + t, rows, :] for t in range(tiles)], axis=1)
            value = dot(gmat[rows, :], mixed[ch]) + base
            value = 0.5 * value * (1.0 + lax.erf(value * (0.5**0.5)))
            out[pl.ds(b * 32, 32), :, lanes] = value.reshape(32, 8, lc).astype(BF16)
            return carry

        lax.fori_loop(0, 4, finish, 0, unroll=True)

    def wait_sends(c):
        for ch in range(nch):
            for j in range(ny):
                c_copy(ch, j, 1 - c).wait_send()
                f_copy(ch, j, c).wait_send()
            for j in range(1, ny):
                r_copy(ch, j, c).wait_send()
                a_copy(ch, j, c).wait_send()

    for c in range(2):
        pl.when(core == c)(functools.partial(wait_sends, c))

    for (there, _, _, _), y_copy, k_copy in zip(pairs, y_copies, k_copies):

        @pl.when(there)
        def _(y_copy=y_copy, k_copy=k_copy):
            y_copy.wait_send()
            k_copy.wait_send()


def shards(field, conv_weight, conv_bias, spectral_weight):
    cells_x, cells_y, width = field.shape
    groups = lax.axis_size("gx")
    modes = spectral_weight.shape[0]
    ny = groups // 2
    lc = width // CHUNKS
    ftab, itab = expanded_tables(cells_x * groups, modes, groups, cells_y)
    dma = pltpu.SemaphoreType.DMA
    vmem = pltpu.VMEM
    scratch = [
        vmem((3, cells_x + 2, cells_y, width), BF16),
        vmem((64, 1024), BF16),
        vmem((27, 32, 32), BF16),
        vmem((8, 2, 32, 32), BF16),
        vmem((1, 32), F32),
        vmem((512, 1024), BF16),
        vmem((1024, 512), BF16),
        vmem((864, 256), F32),
        vmem((2304, 256), BF16),
        vmem((2304, 256), BF16),
        vmem((8, 256, 256), BF16),
        vmem((4, 1024, 128), F32),
        vmem((CHUNKS, 512, lc), F32),
        vmem((CHUNKS, 512, lc), BF16),
        vmem((CHUNKS, 512, lc), BF16),
        vmem((CHUNKS, ny - 1, 128, lc), BF16),
        vmem((CHUNKS, 512, lc), BF16),
        vmem((2, 128, 512), BF16),
        vmem((2, 128, 512), BF16),
        vmem((2, 2, 8, 512), BF16),
        vmem((2, 2, 2, 8, 512), BF16),
        dma((6,)), dma((1,)),
        dma((CHUNKS, ny)), dma((CHUNKS, ny)),
        dma((CHUNKS, ny - 1)), dma((CHUNKS, ny - 1)),
        dma((CHUNKS, ny - 1)), dma((CHUNKS, ny - 1)),
        dma((CHUNKS, ny)), dma((CHUNKS, ny)),
        dma((2,)), dma((2,)), dma((2,)), dma((2,)), dma((2,)), dma((2,)),
        pltpu.SemaphoreType.REGULAR((2,)),
    ]
    operands = (field, conv_weight, conv_bias.reshape(1, -1), spectral_weight, ftab, itab)
    in_hbm = pl.BlockSpec(memory_space=pltpu.HBM)
    return pl.pallas_call(
        layer_kernel,
        out_shape=jax.ShapeDtypeStruct(field.shape, BF16),
        in_specs=[in_hbm] * 6,
        out_specs=pl.BlockSpec(memory_space=pltpu.VMEM),
        scratch_shapes=scratch,
        compiler_params=pltpu.CompilerParams(
            collective_id=0, has_side_effects=True, vmem_limit_bytes=40 * 1024 * 1024
        ),
        name="layer",
    )(*(pltpu.with_memory_space_constraint(a, pltpu.HBM) for a in operands))


def solution(mesh):
    placed = (P("gx", "gy", None), P(), P(), P())
    return jax.shard_map(
        shards, mesh=mesh, in_specs=placed, out_specs=P("gx", "gy", None), check_vma=False
    )
```
